128 devices in a mesh: rep: 32 (over z, y, core), head: 4 (over x).
Axes of the slice: x: 4, y: 4, z: 4, core: 2. Of those that a mesh axis runs over, the one named last changes fastest.
Arguments:
- query_latent: bfloat16 [4, 160, 1536], P(None, 'rep'), may hold values from -48 to 48
- new_entry: bfloat16 [4, 160, 576], P(None, 'rep'), may hold values from -6 to 6
- cache_latent: bfloat16 [10240, 64, 512], P('rep'), may hold values from -6 to 6
- cache_rope: bfloat16 [10240, 4096], P('rep'), may hold values from -6 to 6
- block_table: int32 [160, 64], P('rep'), may hold values from 0 to 319, as said below
- context_len: int32 [160], P('rep'), may hold values from 512 to 4092, as said below
- owner_rows: int32 [32], replicated, may hold values from 0 to 31, each once
- query_up: bfloat16 [1536, 12288], P(('rep', 'head')), may hold values from -0.15625 to 0.15625
- key_up: bfloat16 [512, 8192], P(('rep', 'head')), may hold values from -0.75 to 0.75
- value_up: bfloat16 [512, 8192], P(('rep', 'head')), may hold values from -1 to 1
Outputs:
- attention_out: bfloat16 [4, 160, 8192], P(None, 'rep', 'head')
The draws below stay inside these ranges and needn't reach their ends.
Inputs may be any that keep to these rules, and one draw needn't show every extreme that they name: `block_table`: within each replica the block tables of its 5 requests name every page of its pool once. `context_len`: every replica has a request of length 4092. `owner_rows`: A permutation.
All inputs are finite; a program needn't handle non-finite values.
Results may differ from the reference program's by a relative error of at most 0.035.
Values may be sent and summed in bfloat16 or wider, within the bound.
A program may use at most 192 MiB of HBM per device.

```python
import jax
import jax.numpy as jnp
from jax import lax

H = 64
QR = 1536
LAT = 512
DN = 128
DR = 64
PAGE = 64
MAXP = 64
STEPS = 4
REQ = 5
CTX = 4096
POOL = 320
REQUESTS = 160
QB = 48
N_REP = 32


def draw_query_latent(key, part):
    key = jax.random.fold_in(key, 37)
    base_key, strong_key, pick_key = jax.random.split(key, 3)
    shape = (STEPS, REQUESTS, QR)
    base = jnp.clip(jax.random.normal(base_key, shape, jnp.float32), -6.0, 6.0)
    strong = jax.random.uniform(strong_key, shape, jnp.float32, -1.0, 1.0)
    pick = jax.random.randint(pick_key, (STEPS, REQUESTS, 1), 0, 16)
    strength = jnp.where(pick == 0, 48.0, jnp.where(pick == 1, 24.0, 12.0))
    values = jnp.where(pick < 3, strength * strong, base)
    return values.astype(jnp.bfloat16)


def draw_context_len(key, part):
    key = jax.random.fold_in(key, 11)
    length_key, pick_key = jax.random.split(key)
    replicas = REQUESTS // REQ
    lengths = jax.random.randint(length_key, (replicas, REQ), CTX // 8, CTX - STEPS + 1)
    longest = jax.random.randint(pick_key, (replicas, 1), 0, REQ)
    request_slot = jnp.arange(REQ, dtype=jnp.int32)[None, :]
    lengths = jnp.where(request_slot == longest, CTX - STEPS, lengths)
    return lengths.reshape(REQUESTS).astype(jnp.int32)


def draw_block_table(key, part):
    key = jax.random.fold_in(key, 23)
    replicas = REQUESTS // REQ
    replica_keys = jax.random.split(key, replicas)
    tables = jax.vmap(lambda one_key: jax.random.permutation(one_key, REQ * MAXP))(replica_keys)
    return tables.reshape(REQUESTS, MAXP).astype(jnp.int32)


def levels(rng, shape, shards, low, high):
    loudness, own = 1.0, jax.random.fold_in(rng, 6)
    for position, blocks in shards:
        steps = jnp.exp(jax.random.uniform(jax.random.fold_in(own, position), (blocks,), jnp.float32, low / len(shards), high / len(shards)))
        loudness = loudness * jnp.repeat(steps, shape[position] // blocks).reshape([-1 if axis == position else 1 for axis in range(len(shape))])
    return loudness


def gaussian(own_key, shape, spread, reach, pieces=(), kind=jnp.bfloat16):
    drawn = spread * jax.random.normal(own_key, shape, jnp.float32)
    if pieces:
        drawn = drawn * levels(own_key, shape, pieces, -0.22, 0.18)
    return jnp.clip(drawn, -reach, reach).astype(kind)


def setup_inputs(seed: int = 0) -> dict:
    arg_keys = jax.random.split(jax.random.key(seed), 11)
    query_latent = draw_query_latent(jax.random.fold_in(arg_keys[10], 71), 0)
    new_entry = gaussian(arg_keys[1], (STEPS, REQUESTS, LAT + DR), 1.0, 6.0, ((1, 32),))
    cache_latent = gaussian(arg_keys[2], (REQUESTS * MAXP, PAGE, LAT), 1.0, 6.0, ((0, 32),))
    cache_rope = gaussian(arg_keys[3], (REQUESTS * MAXP, PAGE * DR), 1.0, 6.0, ((0, 32),))
    block_table = draw_block_table(jax.random.fold_in(arg_keys[10], 71), 0)
    context_len = draw_context_len(jax.random.fold_in(arg_keys[10], 71), 0)
    owner_rows = jax.random.permutation(arg_keys[6], N_REP).astype(jnp.int32)
    query_up = gaussian(arg_keys[7], (QR, H * (DN + DR)), QR ** -0.5, 0.15625, ((0, 128),))
    key_up = gaussian(arg_keys[8], (LAT, H * DN), (LAT // 9) ** -0.5, 0.75, ((0, 128),))
    value_up = gaussian(arg_keys[9], (LAT, H * DN), (LAT // 16) ** -0.5, 1.0, ((0, 128),))
    return dict(query_latent=query_latent, new_entry=new_entry, cache_latent=cache_latent, cache_rope=cache_rope, block_table=block_table, context_len=context_len, owner_rows=owner_rows, query_up=query_up, key_up=key_up, value_up=value_up)


def rotate_pairs(values, positions):
    half_width = values.shape[-1] // 2
    frequency = 10000.0 ** (-jnp.arange(half_width, dtype=jnp.float32) / half_width)
    angles = positions[..., None].astype(jnp.float32) * frequency
    lower_half = values[..., :half_width]
    upper_half = values[..., half_width:]
    cosine = jnp.cos(angles)
    sine = jnp.sin(angles)
    return jnp.concatenate([lower_half * cosine - upper_half * sine, upper_half * cosine + lower_half * sine], axis=-1)


def attend_request(query_lat, query_rot, latent, rotary, new_lat, new_rot, length):
    highest = lax.Precision.HIGHEST
    score_scale = (DN + DR) ** -0.5
    query_lat = query_lat.astype(jnp.float32)
    query_rot = query_rot.astype(jnp.float32)
    latent = latent.astype(jnp.float32)
    new_lat = new_lat.astype(jnp.float32)
    cached_scores = jnp.einsum("shl,tl->sht", query_lat, latent, precision=highest)
    cached_scores = cached_scores + jnp.einsum("shc,tc->sht", query_rot, rotary.astype(jnp.float32), precision=highest)
    cached_scores = cached_scores * score_scale
    token_index = jnp.arange(latent.shape[0], dtype=jnp.int32)
    cached_scores = jnp.where(token_index[None, None, :] < length, cached_scores, -1e30)
    fresh_scores = jnp.einsum("shl,ul->shu", query_lat, new_lat, precision=highest)
    fresh_scores = fresh_scores + jnp.einsum("shc,uc->shu", query_rot, new_rot.astype(jnp.float32), precision=highest)
    fresh_scores = fresh_scores * score_scale
    step_index = jnp.arange(new_lat.shape[0], dtype=jnp.int32)
    fresh_scores = jnp.where(step_index[None, None, :] <= step_index[:, None, None], fresh_scores, -1e30)
    scores = jnp.concatenate([cached_scores, fresh_scores], axis=2)
    weights = jax.nn.softmax(scores, axis=2).astype(jnp.bfloat16).astype(jnp.float32)
    cached_count = latent.shape[0]
    mixed_latent = jnp.einsum("sht,tl->shl", weights[:, :, :cached_count], latent, precision=highest)
    mixed_latent = mixed_latent + jnp.einsum("shu,ul->shl", weights[:, :, cached_count:], new_lat, precision=highest)
    return mixed_latent.astype(jnp.bfloat16)


def reference(query_latent, new_entry, cache_latent, cache_rope, block_table, context_len, owner_rows, query_up, key_up, value_up):
    highest = lax.Precision.HIGHEST
    head_total = key_up.shape[1] // DN
    blocks = query_up.reshape(N_REP, QB, head_total * (DN + DR))
    query_true = jnp.zeros_like(blocks).at[owner_rows].set(blocks).reshape(QR, head_total, DN + DR)
    key_heads = key_up.reshape(LAT, head_total, DN).astype(jnp.float32)
    absorbed = jnp.einsum("qhd,lhd->qhl", query_true[:, :, :DN].astype(jnp.float32), key_heads, precision=highest)
    latent_query = query_latent.astype(jnp.float32)
    query_lat = jnp.einsum("siq,qhl->sihl", latent_query, absorbed, precision=highest).astype(jnp.bfloat16)
    query_raw = jnp.einsum("siq,qhc->sihc", latent_query, query_true[:, :, DN:].astype(jnp.float32), precision=highest)
    positions = context_len[None, :] + jnp.arange(STEPS, dtype=jnp.int32)[:, None]
    query_rot = rotate_pairs(query_raw, positions[:, :, None]).astype(jnp.bfloat16)
    new_lat = new_entry[:, :, :LAT]
    new_rot = rotate_pairs(new_entry[:, :, LAT:].astype(jnp.float32), positions).astype(jnp.bfloat16)
    replica = jnp.arange(REQUESTS, dtype=jnp.int32) // REQ
    pages = block_table + (replica * POOL)[:, None]

    def one_request(request_items):
        page_ids, length, one_lat, one_rot, fresh_lat, fresh_rot = request_items
        latent = cache_latent[page_ids].reshape(CTX, LAT)
        rotary = cache_rope[page_ids].reshape(CTX, DR)
        return attend_request(one_lat, one_rot, latent, rotary, fresh_lat, fresh_rot, length)

    attended = lax.map(one_request, (pages, context_len, jnp.swapaxes(query_lat, 0, 1), jnp.swapaxes(query_rot, 0, 1), jnp.swapaxes(new_lat, 0, 1), jnp.swapaxes(new_rot, 0, 1)))
    value_heads = value_up.reshape(LAT, head_total, DN).astype(jnp.float32)
    result = jnp.einsum("ishl,lhd->sihd", attended.astype(jnp.float32), value_heads, precision=highest)
    return result.reshape(STEPS, REQUESTS, head_total * DN).astype(jnp.bfloat16)
```

```python
import functools

import jax
import jax.numpy as jnp
import numpy as np
from jax import lax
from jax.experimental import pallas as pl
from jax.experimental.pallas import tpu as pltpu
from jax.sharding import PartitionSpec as P

LAT = 512
DN = 128
DR = 64
STEPS = 4
REQ = 5
POOL = 320
QR = 1536
HEADS = 16
GROUP = 16
REP = 32
XN = 4
TAIL = QR // 4
XW = QR + TAIL
MSG = 96
QW = 896
SCALE = float((DN + DR) ** -0.5 * np.log2(np.e))
NEG = -1e30
MESH = pl.DeviceIdType.MESH
F32 = jnp.float32
BF16 = jnp.bfloat16
NT = (((1,), (1,)), ((), ()))


def iota(shape, dim):
    return lax.broadcasted_iota(jnp.int32, shape, dim)


def kernel(
    x_ref, ne_ref, lat_hbm, rope_hbm, bt, ln, own, wq_hbm, wk_hbm, wv_hbm, freq_ref, out_ref,
    pool, zpool, rope, wx, kx, vx, wf, kf, msend, mrecv, vfull, xs, xsend, xrecv, xexp, wall,
    qsend, qrecv, wqt, s_a, s_b, m_sc, l_sc, acc, att, nef, cs, pick, outf, inv,
    sem_local, sem_own, a_send, a_recv, x_send, x_recv, xc_sem, m_send, m_recv,
    v_send, v_recv, vc_sem, q_send, q_recv,
):
    r = lax.axis_index("rep")
    hx = lax.axis_index("head")
    core = lax.rem(r, 2)
    chip = r // 2
    base = (r // GROUP) * GROUP
    mine = lax.rem(r, GROUP)
    cell = mine // 2
    other = r + 1 - 2 * core

    rope_copy = pltpu.make_async_copy(rope_hbm, rope, sem_local.at[0])
    rope_copy.start()
    pool_copy = pltpu.make_async_copy(lat_hbm, pool, sem_local.at[1])
    pool_copy.start()

    barrier = pltpu.get_barrier_semaphore()
    for k in range(1, XN):
        pl.semaphore_signal(barrier, inc=1, device_id={"head": lax.rem(hx + k, XN)}, device_id_type=MESH)

    def greet(k, _):
        pl.semaphore_signal(barrier, inc=1, device_id={"rep": lax.rem(r + k, REP)}, device_id_type=MESH)
        return 0

    lax.fori_loop(1, REP, greet, 0)

    for s in range(STEPS):
        row = x_ref[s].astype(F32)
        for i in range(4):
            xs[i * 4 + s : i * 4 + s + 1, :QR] = row[i : i + 1]
        for j in range(4):
            xs[4 * j + s : 4 * j + s + 1, QR:] = row[4:5, TAIL * j : TAIL * (j + 1)]
    xsend[...] = xs[...].astype(BF16)

    pl.semaphore_wait(barrier, XN - 1 + REP - 1)

    parts = ((wq_hbm, wx, 3072), (wk_hbm, kx, 2048), (wv_hbm, vx, 2048))

    def a_copy(n, k):
        src, dst, width = parts[n]
        to = lax.rem(hx + k, XN)
        return pltpu.make_async_remote_copy(
            src_ref=src.at[:, pl.ds(pl.multiple_of(to * width, 128), width)],
            dst_ref=dst.at[hx],
            send_sem=a_send.at[n, k],
            recv_sem=a_recv.at[n, hx],
            device_id={"head": to},
            device_id_type=MESH,
        )

    def a_wait(n, k):
        src, dst, width = parts[n]
        frm = lax.rem(hx + k, XN)
        pltpu.make_async_remote_copy(
            src_ref=dst.at[frm], dst_ref=dst.at[frm], send_sem=a_send.at[n, k], recv_sem=a_recv.at[n, frm],
            device_id={"head": frm}, device_id_type=MESH,
        ).wait_recv()

    def own_copy(n):
        src, dst, width = parts[n]
        return pltpu.make_async_copy(
            src.at[:, pl.ds(pl.multiple_of(hx * width, 128), width)], dst.at[hx], sem_own.at[n]
        )

    for n in range(3):
        for k in (2, 1, 3):
            a_copy(n, k).start()
        own_copy(n).start()

    def x_copy(k):
        to = lax.rem(cell + k, 8)
        return pltpu.make_async_remote_copy(
            src_ref=xsend, dst_ref=xrecv.at[cell, core], send_sem=x_send.at[k], recv_sem=x_recv.at[cell],
            device_id={"rep": base + 2 * to + core}, device_id_type=MESH,
        )

    def x_start(k, _):
        x_copy(k).start()
        return 0

    lax.fori_loop(1, 8, x_start, 0)
    xrecv[cell, core] = xsend[...]

    def invert(j, _):
        at = jnp.int32(0)
        for n in range(REP):
            at = jnp.where(own[n] == j, jnp.int32(n), at)
        inv[j] = at
        return 0

    lax.fori_loop(0, REP, invert, 0)

    lane8 = iota((8, 128), 1)
    sub8 = iota((8, 128), 0)
    sign = jnp.where(lax.rem(lane8, DR) < DR // 2, -1.0, 1.0).astype(F32)
    for i in range(REQ):
        angle = (ln[i] + lax.rem(sub8, STEPS)).astype(F32) * freq_ref[...]
        cs[i, 0] = jnp.cos(angle)
        cs[i, 1] = jnp.sin(angle) * sign
    nef[...] = jnp.zeros_like(nef)
    for u in range(STEPS):
        row = ne_ref[u].astype(F32)
        for i in range(REQ):
            nef[i, u : u + 1, : LAT + DR] = row[i : i + 1]
    for i in range(REQ):
        v = nef[i, :, LAT:]
        v = v + pltpu.roll(v, DR, 1)
        v = v * cs[i, 0] + pltpu.roll(v, DR // 2, 1) * cs[i, 1]
        nef[i, :, LAT:] = jnp.where(lane8 < DR, v, 0.0)

    def clear(n, _):
        wqt[n // 9, pl.ds(pl.multiple_of(lax.rem(n, 9) * 256, 256), 256), :] = jnp.zeros((256, 256), BF16)
        return 0

    lax.fori_loop(0, REQ * 9, clear, 0)
    prow = iota((1024, 512), 0)
    pcol = iota((1024, 512), 1)
    pick[...] = jnp.where(
        (pcol // 16 == lax.rem(prow, 64) // 2) & (lax.rem(pcol, 16) == prow // 64), 1.0, 0.0
    ).astype(BF16)

    rope_copy.wait()

    def rope_step(n, _):
        a, b = n // 4, lax.rem(n, 4)
        top = pl.multiple_of(a * 32, 32)
        cat = jnp.concatenate(
            [
                jnp.concatenate(
                    [rope[pl.ds(top, 16), 128 * j : 128 * j + 128], rope[pl.ds(top + 16, 16), 128 * j : 128 * j + 128]],
                    axis=1,
                )
                for j in range(32)
            ],
            axis=0,
        )
        got = jnp.dot(pick[pl.ds(pl.multiple_of(b * 256, 256), 256), :], cat, preferred_element_type=F32)
        keep = (iota((256, 128), 1) < DR) == (lax.rem(iota((256, 128), 0), 2) == 0)
        for g in range(2):
            v = got[:, 128 * g : 128 * g + 128]
            v = jnp.where(keep, v, pltpu.roll(v, DR, 1)).astype(BF16)
            zpool[pl.ds(a * 32 + g * 16 + b * 4, 4)] = v.reshape(4, 64, 128)
        return 0

    lax.fori_loop(0, 40, rope_step, 0)

    for n in range(2):
        own_copy(n).wait()
        for k in range(1, XN):
            a_wait(n, k)
    for k in range(XN):
        wf[12 * k : 12 * k + 12, :] = wx[k].astype(F32)
        kf[4 * k : 4 * k + 4, :] = kx[k].astype(F32)
    low48 = iota((48, 128), 1) < DR
    low24 = iota((24, 128), 1) < DR
    for p in range(HEADS // 2):
        first = wf[:, 384 * p : 384 * p + 128]
        mid = wf[:, 384 * p + 128 : 384 * p + 256]
        last = wf[:, 384 * p + 256 : 384 * p + 384]
        mid_r = pltpu.roll(mid, DR, 1)
        last_r = pltpu.roll(last, DR, 1)
        msend[2 * p, 0:48] = first.astype(BF16)
        msend[2 * p + 1, 0:48] = jnp.where(low48, mid_r, last_r).astype(BF16)
        pad = jnp.zeros((8, 128), F32)
        even = jnp.concatenate([jnp.where(low24, mid[:24], mid_r[24:]), pad], axis=0)
        odd = jnp.concatenate([jnp.where(low24, last_r[:24], last[24:]), pad], axis=0)
        msend[2 * p, 64:96] = even.astype(BF16)
        msend[2 * p + 1, 64:96] = odd.astype(BF16)
        for g in range(2):
            h = 2 * p + g
            msend[h, 48:64] = kf[:, 128 * h : 128 * h + 128].astype(BF16)

    def m_copy(k):
        to = lax.rem(r + k, REP)
        return pltpu.make_async_remote_copy(
            src_ref=msend.at[lax.rem(to, GROUP)], dst_ref=mrecv.at[r], send_sem=m_send.at[k], recv_sem=m_recv.at[r],
            device_id={"rep": to}, device_id_type=MESH,
        )

    def m_start(k, _):
        m_copy(k).start()
        return 0

    lax.fori_loop(1, REP, m_start, 0)
    mrecv[r] = msend[mine]

    def x_wait(k, _):
        frm = lax.rem(cell + k, 8)
        pltpu.make_async_remote_copy(
            src_ref=xsend, dst_ref=xrecv.at[frm, core], send_sem=x_send.at[k], recv_sem=x_recv.at[frm],
            device_id={"rep": base + 2 * frm + core}, device_id_type=MESH,
        ).wait_recv()
        return 0

    lax.fori_loop(1, 8, x_wait, 0)
    xc = pltpu.make_async_remote_copy(
        src_ref=xrecv.at[:, core], dst_ref=xrecv.at[:, core], send_sem=xc_sem.at[0], recv_sem=xc_sem.at[1],
        device_id={"rep": other}, device_id_type=MESH,
    )
    xc.start()

    own_copy(2).wait()
    for k in range(1, XN):
        a_wait(2, k)
    for k in range(XN):
        kf[4 * k : 4 * k + 4, :] = vx[k].astype(F32)
    vfull[chip, core] = kf[...].astype(BF16)

    def v_copy(k):
        to = lax.rem(chip + k, 16)
        return pltpu.make_async_remote_copy(
            src_ref=vfull.at[chip, core], dst_ref=vfull.at[chip, core], send_sem=v_send.at[k], recv_sem=v_recv.at[chip],
            device_id={"rep": 2 * to + core}, device_id_type=MESH,
        )

    pltpu.make_async_remote_copy(
        src_ref=xrecv.at[:, 1 - core], dst_ref=xrecv.at[:, 1 - core], send_sem=xc_sem.at[0], recv_sem=xc_sem.at[1],
        device_id={"rep": other}, device_id_type=MESH,
    ).wait_recv()

    def spread(n, _):
        got = xrecv[n // 2, lax.rem(n, 2)]
        xexp[n, 0:16, :] = got[:, :QR]
        for j in range(4):
            mask = jnp.where(iota((16, TAIL), 0) // 4 == j, 1.0, 0.0).astype(BF16)
            xexp[n, 16:32, TAIL * j : TAIL * (j + 1)] = got[:, QR:] * mask
        return 0

    lax.fori_loop(0, GROUP, spread, 0)

    def m_wait(k, _):
        frm = lax.rem(r + k, REP)
        pltpu.make_async_remote_copy(
            src_ref=mrecv.at[frm], dst_ref=mrecv.at[frm], send_sem=m_send.at[k], recv_sem=m_recv.at[frm],
            device_id={"rep": frm}, device_id_type=MESH,
        ).wait_recv()
        return 0

    lax.fori_loop(1, REP, m_wait, 0)

    def place(j, _):
        block = mrecv[inv[j]]
        rows = pl.ds(pl.multiple_of(j * 48, 16), 48)
        wall[rows, 0:128] = block[0:48]
        t = block[64:96].astype(F32)[:24]
        t_r = pltpu.roll(t, DR, 1)
        low = iota((24, 128), 1) < DR
        both = jnp.concatenate([jnp.where(low, t, t_r), jnp.where(low, t_r, t)], axis=0)
        wall[rows, 128:256] = both.astype(BF16)
        return 0

    lax.fori_loop(0, REP, place, 0)

    raw = jnp.dot(xexp[...].reshape(GROUP * 32, QR), wall[...], preferred_element_type=F32).reshape(GROUP, 32, 256)
    tail = raw[:, 16:24] + raw[:, 24:32]
    tail = tail + jnp.concatenate([tail[:, 4:8], tail[:, 0:4]], axis=1)
    main = raw[:, 0:16].reshape(GROUP * 16, 256)
    tail = tail.reshape(GROUP * 8, 256)
    both = jnp.concatenate([main, tail], axis=0)
    nope = both[:, :128]
    hi = nope.astype(BF16)
    lo = (nope - hi.astype(F32)).astype(BF16)
    key = mrecv[:, 48:64, :].reshape(LAT, 128)
    lat = lax.dot_general(
        jnp.concatenate([hi, lo], axis=1), jnp.concatenate([key, key], axis=1), NT, preferred_element_type=F32
    )
    rot = both[:, 128:]
    rot_hi = rot.astype(BF16).astype(F32)
    rot = jnp.where(iota(rot.shape, 1) < DR, rot_hi, rot - rot_hi)
    nmain = GROUP * 16
    qsend[:, :, 0:512] = lat[:nmain].astype(BF16).reshape(GROUP, 16, 512)
    qsend[:, :, 512:640] = rot[:nmain].astype(BF16).reshape(GROUP, 16, 128)
    ltail = lat[nmain:].reshape(GROUP, 8, 512)
    upper = iota((GROUP, 8, 128), 1) < 4
    pair = [
        jnp.where(upper, ltail[:, :, 256 * n : 256 * n + 128], ltail[:, :, 256 * n + 128 : 256 * n + 256])
        for n in range(2)
    ]
    qsend[:, :, 640:768] = jnp.concatenate(pair, axis=1).astype(BF16)
    rtail = rot[nmain:].reshape(GROUP, 8, 128)
    qsend[:, :, 768:896] = jnp.concatenate([rtail, rtail], axis=1).astype(BF16)

    def q_copy(k):
        to = lax.rem(mine + k, GROUP)
        return pltpu.make_async_remote_copy(
            src_ref=qsend.at[to], dst_ref=qrecv.at[mine], send_sem=q_send.at[k], recv_sem=q_recv.at[mine],
            device_id={"rep": base + to}, device_id_type=MESH,
        )

    def q_start(k, _):
        q_copy(k).start()
        return 0

    lax.fori_loop(1, GROUP, q_start, 0)
    qrecv[mine] = qsend[mine]

    def v_start(k, _):
        v_copy(k).start()
        return 0

    lax.fori_loop(1, 16, v_start, 0)

    perm_row = iota((256, 256), 0)
    want = lax.rem(perm_row // 4, 16) * 16 + (perm_row // 64) * 4 + lax.rem(perm_row, 4)
    perm = jnp.where(iota((256, 256), 1) == want, 1.0, 0.0).astype(BF16)

    def q_wait(k, _):
        frm = lax.rem(mine + k, GROUP)
        pltpu.make_async_remote_copy(
            src_ref=qsend.at[frm], dst_ref=qrecv.at[frm], send_sem=q_send.at[k], recv_sem=q_recv.at[frm],
            device_id={"rep": base + frm}, device_id_type=MESH,
        ).wait_recv()
        return 0

    lax.fori_loop(1, GROUP, q_wait, 0)

    low_q = iota((LAT, 128), 1) < DR
    low_r = iota((DR, 128), 1) < DR
    got = jnp.dot(perm, qrecv[...].reshape(GROUP * 16, QW), preferred_element_type=F32)
    for i in range(REQ):
        if i < 4:
            lat_i = got[64 * i : 64 * i + 64, :512]
            rp = got[64 * i : 64 * i + 64, 512:640]
        else:
            lat_i = jnp.concatenate([got[64 * j : 64 * j + 64, 640:768] for j in range(4)], axis=1)
            rp = got[0:64, 768:896]
        rr = rp + pltpu.roll(rp, DR, 1)
        cos = jnp.concatenate([cs[i, 0]] * 8, axis=0)
        sin = jnp.concatenate([cs[i, 1]] * 8, axis=0)
        rr = rr * cos + pltpu.roll(rr, DR // 2, 1) * sin
        lat_t = jnp.transpose(jnp.concatenate([lat_i, lat_i], axis=0))
        rr_t = jnp.transpose(jnp.concatenate([rr, rr], axis=0))[:DR]
        left = jnp.where(low_q, lat_t, 0.0).astype(BF16)
        right = jnp.where(low_q, 0.0, lat_t).astype(BF16)
        rleft = jnp.where(low_r, rr_t, 0.0).astype(BF16)
        rright = jnp.where(low_r, 0.0, rr_t).astype(BF16)
        wqt[i, 0:512, 0:128] = left
        wqt[i, 512:1024, 0:128] = right
        wqt[i, 1024:1536, 128:256] = left
        wqt[i, 1536:2048, 128:256] = right
        wqt[i, 2048:2112, 0:128] = rleft
        wqt[i, 2112:2176, 0:128] = rright
        wqt[i, 2176:2240, 128:256] = rleft
        wqt[i, 2240:2304, 128:256] = rright

    pool_copy.wait()

    def page(i, c, k, g):
        return bt[i, c * 16 + k * 4 + g]

    def keys(i, c, k):
        return jnp.concatenate([pool[page(i, c, k, g)] for g in range(4)], axis=0)

    def scores(i, buf, slot):
        def chunk(c):
            s = jnp.dot(keys(i, c, 0), wqt[i, 0:512], preferred_element_type=F32)
            for k in range(1, 4):
                s = s + jnp.dot(keys(i, c, k), wqt[i, 512 * k : 512 * k + 512], preferred_element_type=F32)
            low = iota((64, 128), 1) < DR
            rows = []
            for g in range(4):
                rows.append(
                    jnp.concatenate(
                        [
                            jnp.where(low, zpool[page(i, c, 2 * e, g)], zpool[page(i, c, 2 * e + 1, g)])
                            for e in range(2)
                        ],
                        axis=1,
                    )
                )
            s = s + jnp.dot(jnp.concatenate(rows, axis=0), wqt[i, 2048:2304], preferred_element_type=F32)
            token = iota((256, 256), 0) + (iota((256, 256), 1) // 64) * 256
            s = jnp.where(token < ln[i] - c * 1024, s, NEG)
            buf[pl.ds(pl.multiple_of(c * 256, 256), 256), :] = s
            m_sc[slot] = jnp.maximum(m_sc[slot], jnp.max(s.reshape(32, 8, 256), axis=0))

        return chunk

    def fresh(i, buf, slot):
        new = jnp.concatenate([nef[i], jnp.zeros((8, 640), F32)], axis=0).astype(BF16)
        s = jnp.dot(new[:, :LAT], wqt[i, 0:512], preferred_element_type=F32)
        s = s + jnp.dot(new[:, LAT:], wqt[i, 2048:2176], preferred_element_type=F32)
        u = iota((16, 256), 0)
        lane = iota((16, 256), 1)
        s = jnp.where((lane < 64) & (u <= lax.rem(lane, STEPS)), s, NEG)
        buf[1024:1040, :] = s
        m_sc[slot] = jnp.maximum(s[0:8], s[8:16])

    def top(slot):
        m = jnp.max(m_sc[slot], axis=0, keepdims=True)
        m = jnp.broadcast_to(m, (8, 256))
        m = jnp.maximum(m, pltpu.roll(m, 128, 1))
        m = jnp.maximum(m, pltpu.roll(m, 64, 1))
        return m

    def weigh(i, buf, slot):
        def chunk(c):
            s = buf[pl.ds(pl.multiple_of(c * 256, 256), 256), :]
            p = jnp.exp2((s - m_sc[slot][0:1]) * SCALE)
            l_sc[...] = l_sc[...] + jnp.sum(p.reshape(32, 8, 256), axis=0)
            pt = jnp.transpose(p).astype(BF16)
            t = acc[...]
            for k in range(4):
                t = t + jnp.dot(pt[64 * k : 64 * k + 64], keys(i, c, k), preferred_element_type=F32)
            acc[...] = t

        return chunk

    def weigh_fresh(i, buf, slot):
        s = buf[1024:1040, :]
        p = jnp.exp2((s - m_sc[slot][0:1]) * SCALE)
        l_sc[...] = p[0:8] + p[8:16]
        pt = jnp.transpose(jnp.concatenate([p[:, 0:128], jnp.zeros((112, 128), F32)], axis=0)).astype(BF16)
        new = jnp.concatenate([nef[i, :, :LAT], jnp.zeros((120, LAT), F32)], axis=0).astype(BF16)
        acc[...] = jnp.dot(pt[:64], new, preferred_element_type=F32)

    def finish(i):
        total = jnp.sum(l_sc[...], axis=0, keepdims=True)
        total = jnp.broadcast_to(total, (8, 256))
        total = total + pltpu.roll(total, 128, 1)
        total = total + pltpu.roll(total, 64, 1)
        col = jnp.transpose(jnp.broadcast_to(1.0 / total[0:1, :128], (128, 128)))[:64, 0:1]
        att[i] = acc[...] * col

    def forward():
        def v_wait(k, _):
            frm = lax.rem(chip + k, 16)
            pltpu.make_async_remote_copy(
                src_ref=vfull.at[frm, core], dst_ref=vfull.at[frm, core], send_sem=v_send.at[k],
                recv_sem=v_recv.at[frm], device_id={"rep": 2 * frm + core}, device_id_type=MESH,
            ).wait_recv()
            return 0

        lax.fori_loop(1, 16, v_wait, 0)
        pltpu.make_async_remote_copy(
            src_ref=vfull.at[:, core], dst_ref=vfull.at[:, core], send_sem=vc_sem.at[0], recv_sem=vc_sem.at[1],
            device_id={"rep": other}, device_id_type=MESH,
        ).start()

    bufs = (s_a, s_b)
    for i in range(REQ + 1):
        if i < REQ:
            fresh(i, bufs[i % 2], i % 2)
        if i > 0:
            m_sc[(i - 1) % 2] = top((i - 1) % 2)
            weigh_fresh(i - 1, bufs[(i - 1) % 2], (i - 1) % 2)

        def step(c, _, i=i):
            if i < REQ:
                scores(i, bufs[i % 2], i % 2)(c)
            if i > 0:
                weigh(i - 1, bufs[(i - 1) % 2], (i - 1) % 2)(c)
            return 0

        lax.fori_loop(0, 4, step, 0)
        if i > 0:
            finish(i - 1)
        if i == 3:
            forward()

    pltpu.make_async_remote_copy(
        src_ref=vfull.at[:, 1 - core], dst_ref=vfull.at[:, 1 - core], send_sem=vc_sem.at[0], recv_sem=vc_sem.at[1],
        device_id={"rep": other}, device_id_type=MESH,
    ).wait_recv()
    for p in range(HEADS // 2):
        rows = att[:, 8 * p : 8 * p + 8, :].reshape(REQ * 8, LAT).astype(BF16)
        v = vfull[:, :, :, 256 * p : 256 * p + 256].reshape(LAT, 256)
        o = jnp.dot(rows, v, preferred_element_type=F32).reshape(REQ, 8, 256)
        for i in range(REQ):
            for s in range(STEPS):
                outf[s, i : i + 1, 256 * p : 256 * p + 128] = o[i, s : s + 1, 0:128]
                outf[s, i : i + 1, 256 * p + 128 : 256 * p + 256] = o[i, 4 + s : 5 + s, 128:256]
    for s in range(STEPS):
        out_ref[s] = outf[s, 0:REQ].astype(BF16)

    for n in range(3):
        for k in range(1, XN):
            a_copy(n, k).wait_send()

    def drain(k, _):
        x_copy(k).wait_send()
        return 0

    lax.fori_loop(1, 8, drain, 0)
    xc.wait_send()

    def drain_m(k, _):
        m_copy(k).wait_send()
        return 0

    lax.fori_loop(1, REP, drain_m, 0)

    def drain_qv(k, _):
        q_copy(k).wait_send()
        v_copy(k).wait_send()
        return 0

    lax.fori_loop(1, 16, drain_qv, 0)
    pltpu.make_async_remote_copy(
        src_ref=vfull.at[:, core], dst_ref=vfull.at[:, core], send_sem=vc_sem.at[0], recv_sem=vc_sem.at[1],
        device_id={"rep": other}, device_id_type=MESH,
    ).wait_send()


def on_device(query_latent, new_entry, cache_latent, cache_rope, block_table, context_len, owner_rows, query_up, key_up, value_up):
    half = DR // 2
    freq = np.float32(10000.0) ** (-np.arange(half, dtype=np.float32) / np.float32(half))
    freq = jnp.asarray(np.tile(freq, 4).reshape(1, 128).astype(np.float32))
    vmem = pl.BlockSpec(memory_space=pltpu.VMEM)
    smem = pl.BlockSpec(memory_space=pltpu.SMEM)
    hbm = pl.BlockSpec(memory_space=pl.ANY)
    dma = pltpu.SemaphoreType.DMA
    return pl.pallas_call(
        kernel,
        out_shape=jax.ShapeDtypeStruct((STEPS, REQ, HEADS * DN), BF16),
        in_specs=[vmem, vmem, hbm, hbm, smem, smem, smem, hbm, hbm, hbm, vmem],
        out_specs=vmem,
        scratch_shapes=[
            pltpu.VMEM((POOL, 64, LAT), BF16),
            pltpu.VMEM((POOL, 64, 128), BF16),
            pltpu.VMEM((POOL, 4096), BF16),
            pltpu.VMEM((XN, 12, 3072), BF16),
            pltpu.VMEM((XN, 4, 2048), BF16),
            pltpu.VMEM((XN, 4, 2048), BF16),
            pltpu.VMEM((48, 3072), F32),
            pltpu.VMEM((16, 2048), F32),
            pltpu.VMEM((HEADS, MSG, 128), BF16),
            pltpu.VMEM((REP, MSG, 128), BF16),
            pltpu.VMEM((16, 2, 16, 2048), BF16),
            pltpu.VMEM((16, XW), F32),
            pltpu.VMEM((16, XW), BF16),
            pltpu.VMEM((8, 2, 16, XW), BF16),
            pltpu.VMEM((GROUP, 32, QR), BF16),
            pltpu.VMEM((QR, 256), BF16),
            pltpu.VMEM((GROUP, 16, QW), BF16),
            pltpu.VMEM((GROUP, 16, QW), BF16),
            pltpu.VMEM((REQ, 2304, 256), BF16),
            pltpu.VMEM((1040, 256), F32),
            pltpu.VMEM((1040, 256), F32),
            pltpu.VMEM((2, 8, 256), F32),
            pltpu.VMEM((8, 256), F32),
            pltpu.VMEM((64, LAT), F32),
            pltpu.VMEM((REQ, 64, LAT), F32),
            pltpu.VMEM((REQ, 8, 640), F32),
            pltpu.VMEM((REQ, 2, 8, 128), F32),
            pltpu.VMEM((1024, 512), BF16),
            pltpu.VMEM((STEPS, 8, HEADS * DN), F32),
            pltpu.SMEM((REP,), jnp.int32),
            dma((2,)), dma((3,)), dma((3, XN)), dma((3, XN)),
            dma((8,)), dma((8,)), dma((2,)), dma((REP,)), dma((REP,)),
            dma((16,)), dma((16,)), dma((2,)), dma((GROUP,)), dma((GROUP,)),
        ],
        compiler_params=pltpu.CompilerParams(
            collective_id=0, has_side_effects=True, vmem_limit_bytes=60 * 2**20
        ),
        name="latent_attention",
    )(query_latent, new_entry, cache_latent, cache_rope, block_table, context_len, owner_rows, query_up, key_up, value_up, freq)


def solution(mesh):
    return jax.shard_map(
        on_device,
        mesh=mesh,
        in_specs=(
            P(None, "rep", None),
            P(None, "rep", None),
            P("rep", None, None),
            P("rep", None),
            P("rep", None),
            P("rep"),
            P(),
            P(("rep", "head"), None),
            P(("rep", "head"), None),
            P(("rep", "head"), None),
        ),
        out_specs=P(None, "rep", "head"),
        check_vma=False,
    )
```

```python
import functools

import jax
import jax.numpy as jnp
import numpy as np
from jax import lax
from jax.experimental import pallas as pl
from jax.experimental.pallas import tpu as pltpu
from jax.sharding import PartitionSpec as P

LAT = 512
DN = 128
DR = 64
STEPS = 4
REQ = 5
POOL = 320
QR = 1536
HEADS = 16
GROUP = 16
REP = 32
XN = 4
TAIL = QR // 4
XW = QR + TAIL
MSG = 96
QW = 896
SCALE = float((DN + DR) ** -0.5 * np.log2(np.e))
NEG = -1e30
UNROLL = 2
MESH = pl.DeviceIdType.MESH
F32 = jnp.float32
BF16 = jnp.bfloat16
NT = (((1,), (1,)), ((), ()))


def iota(shape, dim):
    return lax.broadcasted_iota(jnp.int32, shape, dim)


def kernel(
    x_ref, ne_ref, lat_hbm, rope_hbm, bt, ln, own, wq_hbm, wk_hbm, wv_hbm, freq_ref, out_ref,
    pool, zpool, rope, wx, kx, vx, wf, kf, msend, mrecv, vfull, xs, xsend, xrecv, xexp, wall,
    qsend, qrecv, wqt, s_a, s_b, m_sc, l_sc, acc, att, nef, cs, pick, inv,
    sem_local, sem_own, a_send, a_recv, x_send, x_recv, xc_sem, m_send, m_recv,
    v_send, v_recv, vc_sem, q_send, q_recv,
):
    r = lax.axis_index("rep")
    hx = lax.axis_index("head")
    core = lax.rem(r, 2)
    zc = r // 8
    yc = lax.rem(r // 2, 4)
    base = (r // GROUP) * GROUP
    mine = lax.rem(r, GROUP)
    cell = mine // 2
    other = r + 1 - 2 * core

    rope_copy = pltpu.make_async_copy(rope_hbm, rope, sem_local.at[0])
    rope_copy.start()
    pool_copy = pltpu.make_async_copy(lat_hbm, pool, sem_local.at[1])
    pool_copy.start()

    barrier = pltpu.get_barrier_semaphore()
    for k in range(1, XN):
        pl.semaphore_signal(barrier, inc=1, device_id={"head": lax.rem(hx + k, XN)}, device_id_type=MESH)

    def greet(k, _):
        pl.semaphore_signal(barrier, inc=1, device_id={"rep": lax.rem(r + k, REP)}, device_id_type=MESH)
        return 0

    lax.fori_loop(1, REP, greet, 0)

    for i in range(4):
        xs[4 * i : 4 * i + 4, :QR] = x_ref[i].astype(F32)
    row = x_ref[4].astype(F32)
    for j in range(4):
        xs[4 * j : 4 * j + 4, QR:] = row[:, TAIL * j : TAIL * (j + 1)]
    xsend[...] = xs[...].astype(BF16)

    pl.semaphore_wait(barrier, XN - 1 + REP - 1)

    parts = ((wq_hbm, wx, 3072), (wk_hbm, kx, 2048), (wv_hbm, vx, 2048))

    def a_copy(n, k):
        src, dst, width = parts[n]
        to = lax.rem(hx + k, XN)
        return pltpu.make_async_remote_copy(
            src_ref=src.at[:, pl.ds(pl.multiple_of(to * width, 128), width)],
            dst_ref=dst.at[hx],
            send_sem=a_send.at[n, k],
            recv_sem=a_recv.at[n, hx],
            device_id={"head": to},
            device_id_type=MESH,
        )

    def a_wait(n, k):
        src, dst, width = parts[n]
        frm = lax.rem(hx + k, XN)
        pltpu.make_async_remote_copy(
            src_ref=dst.at[frm], dst_ref=dst.at[frm], send_sem=a_send.at[n, k], recv_sem=a_recv.at[n, frm],
            device_id={"head": frm}, device_id_type=MESH,
        ).wait_recv()

    def own_copy(n):
        src, dst, width = parts[n]
        return pltpu.make_async_copy(
            src.at[:, pl.ds(pl.multiple_of(hx * width, 128), width)], dst.at[hx], sem_own.at[n]
        )

    for n in range(3):
        for k in (2, 1, 3):
            a_copy(n, k).start()
        own_copy(n).start()

    def x_copy(k):
        to = lax.rem(cell + k, 8)
        return pltpu.make_async_remote_copy(
            src_ref=xsend, dst_ref=xrecv.at[cell, core], send_sem=x_send.at[k], recv_sem=x_recv.at[cell],
            device_id={"rep": base + 2 * to + core}, device_id_type=MESH,
        )

    def x_start(k, _):
        x_copy(k).start()
        return 0

    lax.fori_loop(1, 8, x_start, 0)
    xrecv[cell, core] = xsend[...]

    def invert(j, _):
        at = jnp.int32(0)
        for n in range(REP):
            at = jnp.where(own[n] == j, jnp.int32(n), at)
        inv[j] = at
        return 0

    lax.fori_loop(0, REP, invert, 0)

    lane8 = iota((8, 128), 1)
    sub8 = iota((8, 128), 0)
    sign = jnp.where(lax.rem(lane8, DR) < DR // 2, -1.0, 1.0).astype(F32)
    for i in range(REQ):
        angle = (ln[i] + lax.rem(sub8, STEPS)).astype(F32) * freq_ref[...]
        cs[i, 0] = jnp.cos(angle)
        cs[i, 1] = jnp.sin(angle) * sign
    nef[...] = jnp.zeros_like(nef)
    for i in range(REQ):
        nef[i, 0:STEPS, : LAT + DR] = ne_ref[i].astype(F32)
        v = nef[i, :, LAT:]
        v = v + pltpu.roll(v, DR, 1)
        v = v * cs[i, 0] + pltpu.roll(v, DR // 2, 1) * cs[i, 1]
        nef[i, :, LAT:] = jnp.where(lane8 < DR, v, 0.0)

    def clear(n, _):
        wqt[n // 9, pl.ds(pl.multiple_of(lax.rem(n, 9) * 256, 256), 256), :] = jnp.zeros((256, 256), BF16)
        return 0

    lax.fori_loop(0, REQ * 9, clear, 0)
    prow = iota((1024, 512), 0)
    pcol = iota((1024, 512), 1)
    pick[...] = jnp.where(
        (pcol // 16 == lax.rem(prow, 64) // 2) & (lax.rem(pcol, 16) == prow // 64), 1.0, 0.0
    ).astype(BF16)

    for n in range(2):
        own_copy(n).wait()
        for k in range(1, XN):
            a_wait(n, k)
    for k in range(XN):
        wf[12 * k : 12 * k + 12, :] = wx[k].astype(F32)
        kf[4 * k : 4 * k + 4, :] = kx[k].astype(F32)
    low48 = iota((48, 128), 1) < DR
    low24 = iota((24, 128), 1) < DR

    def m_copy(h, half):
        to = half * GROUP + h
        return to, pltpu.make_async_remote_copy(
            src_ref=msend.at[h], dst_ref=mrecv.at[r], send_sem=m_send.at[to], recv_sem=m_recv.at[r],
            device_id={"rep": to}, device_id_type=MESH,
        )

    def make(k, _):
        p = lax.rem(cell + k, HEADS // 2)
        col = pl.multiple_of(p * 384, 128)
        first = wf[:, pl.ds(col, 128)]
        mid = wf[:, pl.ds(pl.multiple_of(col + 128, 128), 128)]
        last = wf[:, pl.ds(pl.multiple_of(col + 256, 128), 128)]
        mid_r = pltpu.roll(mid, DR, 1)
        last_r = pltpu.roll(last, DR, 1)
        pad = jnp.zeros((8, 128), F32)
        even = jnp.concatenate([jnp.where(low24, mid[:24], mid_r[24:]), pad], axis=0)
        odd = jnp.concatenate([jnp.where(low24, last_r[:24], last[24:]), pad], axis=0)
        msend[2 * p, 0:48] = first.astype(BF16)
        msend[2 * p, 48:64] = kf[:, pl.ds(pl.multiple_of(p * 256, 128), 128)].astype(BF16)
        msend[2 * p, 64:96] = even.astype(BF16)
        msend[2 * p + 1, 0:48] = jnp.where(low48, mid_r, last_r).astype(BF16)
        msend[2 * p + 1, 48:64] = kf[:, pl.ds(pl.multiple_of(p * 256 + 128, 128), 128)].astype(BF16)
        msend[2 * p + 1, 64:96] = odd.astype(BF16)
        for g in range(2):
            for half in range(2):
                to, copy = m_copy(2 * p + g, half)

                @pl.when(to != r)
                def _(copy=copy):
                    copy.start()

        return 0

    lax.fori_loop(0, HEADS // 2, make, 0)
    mrecv[r] = msend[mine]

    def x_wait(k, _):
        frm = lax.rem(cell + k, 8)
        pltpu.make_async_remote_copy(
            src_ref=xsend, dst_ref=xrecv.at[frm, core], send_sem=x_send.at[k], recv_sem=x_recv.at[frm],
            device_id={"rep": base + 2 * frm + core}, device_id_type=MESH,
        ).wait_recv()
        return 0

    lax.fori_loop(1, 8, x_wait, 0)
    xc = pltpu.make_async_remote_copy(
        src_ref=xrecv.at[:, core], dst_ref=xrecv.at[:, core], send_sem=xc_sem.at[0], recv_sem=xc_sem.at[1],
        device_id={"rep": other}, device_id_type=MESH,
    )
    xc.start()

    own_copy(2).wait()
    for k in range(1, XN):
        a_wait(2, k)
    for k in range(XN):
        kf[4 * k : 4 * k + 4, :] = vx[k].astype(F32)
    vfull[zc, yc, core] = kf[...].astype(BF16)

    def v_peer(axis, k):
        if axis == 0:
            return lax.rem(zc + k, 4), yc
        return zc, lax.rem(yc + k, 4)

    def v_copy(hop, side, k):
        axis = side if hop == 0 else 1 - side
        to_z, to_y = v_peer(axis, k)
        cols = slice(1024 * side, 1024 * side + 1024)
        if hop == 0:
            block = vfull.at[zc, yc, core, :, cols]
        elif side == 0:
            block = vfull.at[:, yc, core, :, cols]
        else:
            block = vfull.at[zc, :, core, :, cols]
        return pltpu.make_async_remote_copy(
            src_ref=block, dst_ref=block, send_sem=v_send.at[hop, side, k],
            recv_sem=v_recv.at[hop, side, zc if axis == 0 else yc],
            device_id={"rep": to_z * 8 + to_y * 2 + core}, device_id_type=MESH,
        )

    def v_wait(hop, side, k):
        axis = side if hop == 0 else 1 - side
        from_z, from_y = v_peer(axis, k)
        cols = slice(1024 * side, 1024 * side + 1024)
        if hop == 0:
            block = vfull.at[from_z, from_y, core, :, cols]
        elif side == 0:
            block = vfull.at[:, from_y, core, :, cols]
        else:
            block = vfull.at[from_z, :, core, :, cols]
        pltpu.make_async_remote_copy(
            src_ref=block, dst_ref=block, send_sem=v_send.at[hop, side, k],
            recv_sem=v_recv.at[hop, side, from_z if axis == 0 else from_y],
            device_id={"rep": from_z * 8 + from_y * 2 + core}, device_id_type=MESH,
        ).wait_recv()

    def v_start(hop):
        for side in range(2):
            for k in (2, 1, 3):
                v_copy(hop, side, k).start()

    def v_wait_all(hop):
        for side in range(2):
            for k in (1, 3, 2):
                v_wait(hop, side, k)

    v_start(0)

    rope_copy.wait()

    def rope_step(a, _):
        top = pl.multiple_of(a * 32, 32)
        cat = jnp.concatenate(
            [
                jnp.concatenate(
                    [rope[pl.ds(top, 16), 128 * j : 128 * j + 128], rope[pl.ds(top + 16, 16), 128 * j : 128 * j + 128]],
                    axis=1,
                )
                for j in range(32)
            ],
            axis=0,
        )
        keep = (iota((256, 128), 1) < DR) == (lax.rem(iota((256, 128), 0), 2) == 0)
        for b in range(4):
            got = jnp.dot(pick[256 * b : 256 * b + 256, :], cat, preferred_element_type=F32)
            for g in range(2):
                v = got[:, 128 * g : 128 * g + 128]
                v = jnp.where(keep, v, pltpu.roll(v, DR, 1)).astype(BF16)
                zpool[pl.ds(a * 32 + g * 16 + b * 4, 4)] = v.reshape(4, 64, 128)
        return 0

    lax.fori_loop(0, POOL // 32, rope_step, 0)

    pltpu.make_async_remote_copy(
        src_ref=xrecv.at[:, 1 - core], dst_ref=xrecv.at[:, 1 - core], send_sem=xc_sem.at[0], recv_sem=xc_sem.at[1],
        device_id={"rep": other}, device_id_type=MESH,
    ).wait_recv()

    def spread(n, _):
        got = xrecv[n // 2, lax.rem(n, 2)]
        xexp[n, 0:16, :] = got[:, :QR]
        for j in range(4):
            mask = jnp.where(iota((16, TAIL), 0) // 4 == j, 1.0, 0.0).astype(BF16)
            xexp[n, 16:32, TAIL * j : TAIL * (j + 1)] = got[:, QR:] * mask
        return 0

    lax.fori_loop(0, GROUP, spread, 0)

    def m_wait(k, _):
        frm = lax.rem(r + k, REP)
        pltpu.make_async_remote_copy(
            src_ref=mrecv.at[frm], dst_ref=mrecv.at[frm], send_sem=m_send.at[k], recv_sem=m_recv.at[frm],
            device_id={"rep": frm}, device_id_type=MESH,
        ).wait_recv()
        return 0

    lax.fori_loop(1, REP, m_wait, 0)

    def place(j, _):
        block = mrecv[inv[j]]
        rows = pl.ds(pl.multiple_of(j * 48, 16), 48)
        wall[rows, 0:128] = block[0:48]
        t = block[64:96].astype(F32)[:24]
        t_r = pltpu.roll(t, DR, 1)
        low = iota((24, 128), 1) < DR
        both = jnp.concatenate([jnp.where(low, t, t_r), jnp.where(low, t_r, t)], axis=0)
        wall[rows, 128:256] = both.astype(BF16)
        return 0

    lax.fori_loop(0, REP, place, 0)

    key = mrecv[:, 48:64, :].reshape(LAT, 128)
    key = jnp.concatenate([key, key], axis=1)
    half = GROUP // 2

    def q_copy(to):
        return pltpu.make_async_remote_copy(
            src_ref=qsend.at[to], dst_ref=qrecv.at[mine], send_sem=q_send.at[to], recv_sem=q_recv.at[mine],
            device_id={"rep": base + to}, device_id_type=MESH,
        )

    for e in (1, 0):
        group = pl.multiple_of(lax.rem(mine // half + e, 2) * half, half)
        members = pl.ds(group, half)
        raw = jnp.dot(xexp[members].reshape(half * 32, QR), wall[...], preferred_element_type=F32)
        raw = raw.reshape(half, 32, 256)
        tail = raw[:, 16:24] + raw[:, 24:32]
        tail = tail + jnp.concatenate([tail[:, 4:8], tail[:, 0:4]], axis=1)
        both = jnp.concatenate([raw[:, 0:16].reshape(half * 16, 256), tail.reshape(half * 8, 256)], axis=0)
        nope = both[:, :128]
        hi = nope.astype(BF16)
        lo = (nope - hi.astype(F32)).astype(BF16)
        lat = lax.dot_general(jnp.concatenate([hi, lo], axis=1), key, NT, preferred_element_type=F32)
        rot = both[:, 128:]
        rot_hi = rot.astype(BF16).astype(F32)
        rot = jnp.where(iota(rot.shape, 1) < DR, rot_hi, rot - rot_hi)
        nmain = half * 16
        qsend[members, :, 0:512] = lat[:nmain].astype(BF16).reshape(half, 16, 512)
        qsend[members, :, 512:640] = rot[:nmain].astype(BF16).reshape(half, 16, 128)
        ltail = lat[nmain:].reshape(half, 8, 512)
        upper = iota((half, 8, 128), 1) < 4
        pair = [
            jnp.where(upper, ltail[:, :, 256 * n : 256 * n + 128], ltail[:, :, 256 * n + 128 : 256 * n + 256])
            for n in range(2)
        ]
        qsend[members, :, 640:768] = jnp.concatenate(pair, axis=1).astype(BF16)
        rtail = rot[nmain:].reshape(half, 8, 128)
        qsend[members, :, 768:896] = jnp.concatenate([rtail, rtail], axis=1).astype(BF16)

        def q_start(k, _, e=e, group=group):
            q_copy(group + lax.rem(mine + k, half)).start()
            return 0

        lax.fori_loop(1 - e, half, q_start, 0)

    qrecv[mine] = qsend[mine]

    v_wait_all(0)
    v_start(1)

    perm_row = iota((256, 256), 0)
    want = lax.rem(perm_row // 4, 16) * 16 + (perm_row // 64) * 4 + lax.rem(perm_row, 4)
    perm = jnp.where(iota((256, 256), 1) == want, 1.0, 0.0).astype(BF16)

    def q_wait(k, _):
        frm = lax.rem(mine + k, GROUP)
        pltpu.make_async_remote_copy(
            src_ref=qsend.at[frm], dst_ref=qrecv.at[frm], send_sem=q_send.at[k], recv_sem=q_recv.at[frm],
            device_id={"rep": base + frm}, device_id_type=MESH,
        ).wait_recv()
        return 0

    lax.fori_loop(1, GROUP, q_wait, 0)

    low_q = iota((LAT, 128), 1) < DR
    low_r = iota((DR, 128), 1) < DR
    got = jnp.dot(perm, qrecv[...].reshape(GROUP * 16, QW), preferred_element_type=F32)
    for i in range(REQ):
        if i < 4:
            lat_i = got[64 * i : 64 * i + 64, :512]
            rp = got[64 * i : 64 * i + 64, 512:640]
        else:
            lat_i = jnp.concatenate([got[64 * j : 64 * j + 64, 640:768] for j in range(4)], axis=1)
            rp = got[0:64, 768:896]
        rr = rp + pltpu.roll(rp, DR, 1)
        cos = jnp.concatenate([cs[i, 0]] * 8, axis=0)
        sin = jnp.concatenate([cs[i, 1]] * 8, axis=0)
        rr = rr * cos + pltpu.roll(rr, DR // 2, 1) * sin
        lat_t = jnp.transpose(jnp.concatenate([lat_i, lat_i], axis=0))
        rr_t = jnp.transpose(jnp.concatenate([rr, rr], axis=0))[:DR]
        left = jnp.where(low_q, lat_t, 0.0).astype(BF16)
        right = jnp.where(low_q, 0.0, lat_t).astype(BF16)
        rleft = jnp.where(low_r, rr_t, 0.0).astype(BF16)
        rright = jnp.where(low_r, 0.0, rr_t).astype(BF16)
        wqt[i, 0:512, 0:128] = left
        wqt[i, 512:1024, 0:128] = right
        wqt[i, 1024:1536, 128:256] = left
        wqt[i, 1536:2048, 128:256] = right
        wqt[i, 2048:2112, 0:128] = rleft
        wqt[i, 2112:2176, 0:128] = rright
        wqt[i, 2176:2240, 128:256] = rleft
        wqt[i, 2240:2304, 128:256] = rright

    pool_copy.wait()

    def page(i, c, k, g):
        return bt[i, c * 16 + k * 4 + g]

    def keys(i, c, k):
        return jnp.concatenate([pool[page(i, c, k, g)] for g in range(4)], axis=0)

    def scores(i, buf, slot):
        def chunk(c):
            s = jnp.dot(keys(i, c, 0), wqt[i, 0:512], preferred_element_type=F32)
            for k in range(1, 4):
                s = s + jnp.dot(keys(i, c, k), wqt[i, 512 * k : 512 * k + 512], preferred_element_type=F32)
            low = iota((64, 128), 1) < DR
            rows = []
            for g in range(4):
                rows.append(
                    jnp.concatenate(
                        [
                            jnp.where(low, zpool[page(i, c, 2 * e, g)], zpool[page(i, c, 2 * e + 1, g)])
                            for e in range(2)
                        ],
                        axis=1,
                    )
                )
            s = s + jnp.dot(jnp.concatenate(rows, axis=0), wqt[i, 2048:2304], preferred_element_type=F32)
            token = iota((256, 256), 0) + (iota((256, 256), 1) // 64) * 256
            s = jnp.where(token < ln[i] - c * 1024, s, NEG)
            buf[pl.ds(pl.multiple_of(c * 256, 256), 256), :] = s
            m_sc[slot] = jnp.maximum(m_sc[slot], jnp.max(s.reshape(32, 8, 256), axis=0))

        return chunk

    def fresh(i, buf, slot):
        new = jnp.concatenate([nef[i], jnp.zeros((8, 640), F32)], axis=0).astype(BF16)
        s = jnp.dot(new[:, :LAT], wqt[i, 0:512], preferred_element_type=F32)
        s = s + jnp.dot(new[:, LAT:], wqt[i, 2048:2176], preferred_element_type=F32)
        u = iota((16, 256), 0)
        lane = iota((16, 256), 1)
        s = jnp.where((lane < 64) & (u <= lax.rem(lane, STEPS)), s, NEG)
        buf[1024:1040, :] = s
        m_sc[slot] = jnp.maximum(s[0:8], s[8:16])

    def top(slot):
        m = jnp.max(m_sc[slot], axis=0, keepdims=True)
        m = jnp.broadcast_to(m, (8, 256))
        m = jnp.maximum(m, pltpu.roll(m, 128, 1))
        m = jnp.maximum(m, pltpu.roll(m, 64, 1))
        return m

    def weigh(i, buf, slot):
        def chunk(c):
            s = buf[pl.ds(pl.multiple_of(c * 256, 256), 256), :]
            p = jnp.exp2((s - m_sc[slot][0:1]) * SCALE)
            l_sc[...] = l_sc[...] + jnp.sum(p.reshape(32, 8, 256), axis=0)
            pt = jnp.transpose(p).astype(BF16)
            t = acc[...]
            for k in range(4):
                t = t + jnp.dot(pt[64 * k : 64 * k + 64], keys(i, c, k), preferred_element_type=F32)
            acc[...] = t

        return chunk

    def weigh_fresh(i, buf, slot):
        s = buf[1024:1040, :]
        p = jnp.exp2((s - m_sc[slot][0:1]) * SCALE)
        l_sc[...] = p[0:8] + p[8:16]
        pt = jnp.transpose(jnp.concatenate([p[:, 0:128], jnp.zeros((112, 128), F32)], axis=0)).astype(BF16)
        new = jnp.concatenate([nef[i, :, :LAT], jnp.zeros((120, LAT), F32)], axis=0).astype(BF16)
        acc[...] = jnp.dot(pt[:64], new, preferred_element_type=F32)

    def finish(i):
        total = jnp.sum(l_sc[...], axis=0, keepdims=True)
        total = jnp.broadcast_to(total, (8, 256))
        total = total + pltpu.roll(total, 128, 1)
        total = total + pltpu.roll(total, 64, 1)
        col = jnp.transpose(jnp.broadcast_to(1.0 / total[0:1, :128], (128, 128)))[:64, 0:1]
        att[i] = acc[...] * col

    def forward():
        v_wait_all(1)
        pltpu.make_async_remote_copy(
            src_ref=vfull.at[:, :, core], dst_ref=vfull.at[:, :, core], send_sem=vc_sem.at[0], recv_sem=vc_sem.at[1],
            device_id={"rep": other}, device_id_type=MESH,
        ).start()

    bufs = (s_a, s_b)
    for i in range(REQ + 1):
        if i < REQ:
            fresh(i, bufs[i % 2], i % 2)
        if i > 0:
            m_sc[(i - 1) % 2] = top((i - 1) % 2)
            weigh_fresh(i - 1, bufs[(i - 1) % 2], (i - 1) % 2)

        def step(c, _, i=i):
            for d in range(UNROLL):
                if i < REQ:
                    scores(i, bufs[i % 2], i % 2)(c * UNROLL + d)
                if i > 0:
                    weigh(i - 1, bufs[(i - 1) % 2], (i - 1) % 2)(c * UNROLL + d)
            return 0

        lax.fori_loop(0, 4 // UNROLL, step, 0)
        if i > 0:
            finish(i - 1)
        if i == 3:
            forward()

    pltpu.make_async_remote_copy(
        src_ref=vfull.at[:, :, 1 - core], dst_ref=vfull.at[:, :, 1 - core], send_sem=vc_sem.at[0], recv_sem=vc_sem.at[1],
        device_id={"rep": other}, device_id_type=MESH,
    ).wait_recv()
    for p in range(HEADS // 2):
        rows = att[:, 8 * p : 8 * p + 8, :].reshape(REQ * 8, LAT).astype(BF16)
        v = vfull[:, :, :, :, 256 * p : 256 * p + 256].reshape(LAT, 256)
        o = jnp.dot(rows, v, preferred_element_type=F32).reshape(REQ, 8, 256)
        for i in range(REQ):
            out_ref[i, :, 256 * p : 256 * p + 128] = o[i, 0:4, 0:128].astype(BF16)
            out_ref[i, :, 256 * p + 128 : 256 * p + 256] = o[i, 4:8, 128:256].astype(BF16)

    for n in range(3):
        for k in range(1, XN):
            a_copy(n, k).wait_send()

    def drain(k, _):
        x_copy(k).wait_send()
        return 0

    lax.fori_loop(1, 8, drain, 0)
    xc.wait_send()

    def drain_m(k, _):
        to = lax.rem(r + k, REP)
        m_copy(lax.rem(to, GROUP), to // GROUP)[1].wait_send()
        return 0

    lax.fori_loop(1, REP, drain_m, 0)

    def drain_q(k, _):
        q_copy(lax.rem(mine + k, GROUP)).wait_send()
        return 0

    lax.fori_loop(1, GROUP, drain_q, 0)
    for hop in range(2):
        for side in range(2):
            for k in range(1, 4):
                v_copy(hop, side, k).wait_send()
    pltpu.make_async_remote_copy(
        src_ref=vfull.at[:, :, core], dst_ref=vfull.at[:, :, core], send_sem=vc_sem.at[0], recv_sem=vc_sem.at[1],
        device_id={"rep": other}, device_id_type=MESH,
    ).wait_send()


def on_device(query_latent, new_entry, cache_latent, cache_rope, block_table, context_len, owner_rows, query_up, key_up, value_up):
    half = DR // 2
    freq = np.float32(10000.0) ** (-np.arange(half, dtype=np.float32) / np.float32(half))
    freq = jnp.asarray(np.tile(freq, 4).reshape(1, 128).astype(np.float32))
    vmem = pl.BlockSpec(memory_space=pltpu.VMEM)
    smem = pl.BlockSpec(memory_space=pltpu.SMEM)
    hbm = pl.BlockSpec(memory_space=pl.ANY)
    dma = pltpu.SemaphoreType.DMA
    out = pl.pallas_call(
        kernel,
        out_shape=jax.ShapeDtypeStruct((REQ, STEPS, HEADS * DN), BF16),
        in_specs=[vmem, vmem, hbm, hbm, smem, smem, smem, hbm, hbm, hbm, vmem],
        out_specs=vmem,
        scratch_shapes=[
            pltpu.VMEM((POOL, 64, LAT), BF16),
            pltpu.VMEM((POOL, 64, 128), BF16),
            pltpu.VMEM((POOL, 4096), BF16),
            pltpu.VMEM((XN, 12, 3072), BF16),
            pltpu.VMEM((XN, 4, 2048), BF16),
            pltpu.VMEM((XN, 4, 2048), BF16),
            pltpu.VMEM((48, 3072), F32),
            pltpu.VMEM((16, 2048), F32),
            pltpu.VMEM((HEADS, MSG, 128), BF16),
            pltpu.VMEM((REP, MSG, 128), BF16),
            pltpu.VMEM((4, 4, 2, 16, 2048), BF16),
            pltpu.VMEM((16, XW), F32),
            pltpu.VMEM((16, XW), BF16),
            pltpu.VMEM((8, 2, 16, XW), BF16),
            pltpu.VMEM((GROUP, 32, QR), BF16),
            pltpu.VMEM((QR, 256), BF16),
            pltpu.VMEM((GROUP, 16, QW), BF16),
            pltpu.VMEM((GROUP, 16, QW), BF16),
            pltpu.VMEM((REQ, 2304, 256), BF16),
            pltpu.VMEM((1040, 256), F32),
            pltpu.VMEM((1040, 256), F32),
            pltpu.VMEM((2, 8, 256), F32),
            pltpu.VMEM((8, 256), F32),
            pltpu.VMEM((64, LAT), F32),
            pltpu.VMEM((REQ, 64, LAT), F32),
            pltpu.VMEM((REQ, 8, 640), F32),
            pltpu.VMEM((REQ, 2, 8, 128), F32),
            pltpu.VMEM((1024, 512), BF16),
            pltpu.SMEM((REP,), jnp.int32),
            dma((2,)), dma((3,)), dma((3, XN)), dma((3, XN)),
            dma((8,)), dma((8,)), dma((2,)), dma((REP,)), dma((REP,)),
            dma((2, 2, 4)), dma((2, 2, 4)), dma((2,)), dma((GROUP,)), dma((GROUP,)),
        ],
        compiler_params=pltpu.CompilerParams(
            collective_id=0, has_side_effects=True, vmem_limit_bytes=60 * 2**20
        ),
        name="latent_attention",
    )(jnp.swapaxes(query_latent, 0, 1), jnp.swapaxes(new_entry, 0, 1), cache_latent, cache_rope, block_table, context_len, owner_rows, query_up, key_up, value_up, freq)
    return jnp.swapaxes(out, 0, 1)


def solution(mesh):
    return jax.shard_map(
        on_device,
        mesh=mesh,
        in_specs=(
            P(None, "rep", None),
            P(None, "rep", None),
            P("rep", None, None),
            P("rep", None),
            P("rep", None),
            P("rep"),
            P(),
            P(("rep", "head"), None),
            P(("rep", "head"), None),
            P(("rep", "head"), None),
        ),
        out_specs=P(None, "rep", "head"),
        check_vma=False,
    )
```

```python
import functools

import jax
import jax.numpy as jnp
import numpy as np
from jax import lax
from jax.experimental import pallas as pl
from jax.experimental.pallas import tpu as pltpu
from jax.sharding import PartitionSpec as P

LAT = 512
DN = 128
DR = 64
STEPS = 4
REQ = 5
POOL = 320
QR = 1536
HEADS = 16
GROUP = 16
REP = 32
XN = 4
TAIL = QR // 4
XW = QR + TAIL
MSG = 96
SCALE = float((DN + DR) ** -0.5 * np.log2(np.e))
NEG = -1e30
GATHER = 2
MESH = pl.DeviceIdType.MESH
F32 = jnp.float32
BF16 = jnp.bfloat16
NT = (((1,), (1,)), ((), ()))


def iota(shape, dim):
    return lax.broadcasted_iota(jnp.int32, shape, dim)


def kernel(
    x_ref, ne_ref, lat_hbm, rope_hbm, bt, ln, own, wq_hbm, wk_hbm, wv_hbm, freq_ref, out_ref,
    pool, zpool, rope, wx, kx, vx, wf, kf, msend, mrecv, vfull, xs, xsend, xrecv, xexp, wall,
    qsend, qrecv, qsend2, qrecv2, wqt, s_a, s_b, m_sc, l_sc, acc, att, nef, cs, pick, inv,
    sem_local, sem_own, a_send, a_recv, x_send, x_recv, xc_sem, m_send, m_recv,
    v_send, v_recv, vc_sem, q_send, q_recv, row_sem, plane_sem,
):
    r = lax.axis_index("rep")
    hx = lax.axis_index("head")
    core = lax.rem(r, 2)
    zc = r // 8
    yc = lax.rem(r // 2, 4)
    base = (r // GROUP) * GROUP
    mine = lax.rem(r, GROUP)
    cell = mine // 2
    head = core * 8 + cell
    other = r + 1 - 2 * core

    rope_copy = pltpu.make_async_copy(rope_hbm, rope, sem_local.at[0])
    rope_copy.start()
    pool_copy = pltpu.make_async_copy(lat_hbm, pool, sem_local.at[1])
    pool_copy.start()

    def along(axis, k):
        if axis == "x":
            return {"head": lax.rem(hx + k, XN)}
        if axis == "core":
            return {"rep": other}
        if axis == "y":
            return {"rep": zc * 8 + lax.rem(yc + k, 4) * 2 + core}
        return {"rep": lax.rem(zc + k, 4) * 8 + yc * 2 + core}

    barrier = pltpu.get_barrier_semaphore()
    for axis in ("x", "core", "y", "z"):
        for k in range(1, 2 if axis == "core" else 4):
            pl.semaphore_signal(barrier, inc=1, device_id=along(axis, k), device_id_type=MESH)

    pl.semaphore_wait(barrier, 10)

    parts = (
        (wk_hbm, kx, 2048, 0, 2048),
        (wq_hbm, wx, 3072, 0, 1536),
        (wq_hbm, wx, 3072, 1536, 1536),
        (wv_hbm, vx, 2048, 0, 2048),
    )

    def a_source(n, to):
        src, dst, width, first, size = parts[n]
        return src.at[:, pl.ds(pl.multiple_of(to * width + first, 128), size)]

    def a_block(n, frm):
        src, dst, width, first, size = parts[n]
        return dst.at[frm, :, first : first + size]

    def a_copy(n, k):
        to = lax.rem(hx + k, XN)
        return pltpu.make_async_remote_copy(
            src_ref=a_source(n, to), dst_ref=a_block(n, hx), send_sem=a_send.at[n, k], recv_sem=a_recv.at[n, hx],
            device_id={"head": to}, device_id_type=MESH,
        )

    def a_wait(n):
        own_copy(n).wait()
        for k in range(1, XN):
            frm = lax.rem(hx + k, XN)
            pltpu.make_async_remote_copy(
                src_ref=a_block(n, frm), dst_ref=a_block(n, frm), send_sem=a_send.at[n, k], recv_sem=a_recv.at[n, frm],
                device_id={"head": frm}, device_id_type=MESH,
            ).wait_recv()

    def own_copy(n):
        return pltpu.make_async_copy(a_source(n, hx), a_block(n, hx), sem_own.at[n])

    def a_start(n):
        for k in (2, 1, 3):
            a_copy(n, k).start()
        own_copy(n).start()

    for n in range(3):
        a_start(n)
    for k in range(1, 4):
        pl.semaphore_signal(row_sem, inc=1, device_id=along("y", k), device_id_type=MESH)

    for i in range(4):
        xs[4 * i : 4 * i + 4, :QR] = x_ref[i].astype(F32)
    row = x_ref[4].astype(F32)
    for j in range(4):
        xs[4 * j : 4 * j + 4, QR:] = row[:, TAIL * j : TAIL * (j + 1)]
    xsend[...] = xs[...].astype(BF16)

    pl.semaphore_wait(row_sem, 3)
    for k in range(1, 4):
        pl.semaphore_signal(plane_sem, inc=1, device_id=along("z", k), device_id_type=MESH)

    def invert(j, _):
        at = jnp.int32(0)
        for n in range(REP):
            at = jnp.where(own[n] == j, jnp.int32(n), at)
        inv[j] = at
        return 0

    lax.fori_loop(0, REP, invert, 0)

    pl.semaphore_wait(plane_sem, 3)

    def x_copy(k):
        to = lax.rem(cell + k, 8)
        return pltpu.make_async_remote_copy(
            src_ref=xsend, dst_ref=xrecv.at[cell, core], send_sem=x_send.at[k], recv_sem=x_recv.at[cell],
            device_id={"rep": base + 2 * to + core}, device_id_type=MESH,
        )

    def x_start(k, _):
        x_copy(k).start()
        return 0

    lax.fori_loop(1, 8, x_start, 0)
    xrecv[cell, core] = xsend[...]

    lane8 = iota((8, 128), 1)
    sub8 = iota((8, 128), 0)
    sign = jnp.where(lax.rem(lane8, DR) < DR // 2, -1.0, 1.0).astype(F32)
    for i in range(REQ):
        angle = (ln[i] + lax.rem(sub8, STEPS)).astype(F32) * freq_ref[...]
        cs[i, 0] = jnp.cos(angle)
        cs[i, 1] = jnp.sin(angle) * sign
    nef[...] = jnp.zeros_like(nef)
    for i in range(REQ):
        nef[i, 0:STEPS, : LAT + DR] = ne_ref[i].astype(F32)
        v = nef[i, :, LAT:]
        v = v + pltpu.roll(v, DR, 1)
        v = v * cs[i, 0] + pltpu.roll(v, DR // 2, 1) * cs[i, 1]
        nef[i, :, LAT:] = jnp.where(lane8 < DR, v, 0.0)

    def clear(n, _):
        wqt[n // 9, pl.ds(pl.multiple_of(lax.rem(n, 9) * 256, 256), 256), :] = jnp.zeros((256, 256), BF16)
        return 0

    lax.fori_loop(0, REQ * 9, clear, 0)
    prow = iota((1024, 512), 0)
    pcol = iota((1024, 512), 1)
    pick[...] = jnp.where(
        (pcol // 16 == lax.rem(prow, 64) // 2) & (lax.rem(pcol, 16) == prow // 64), 1.0, 0.0
    ).astype(BF16)

    a_wait(0)
    for k in range(XN):
        kf[4 * k : 4 * k + 4, :] = kx[k].astype(F32)
    low48 = iota((48, 128), 1) < DR
    low24 = iota((24, 128), 1) < DR

    def m_copy(h, half):
        to = half * GROUP + lax.rem(h, 8) * 2 + h // 8
        return to, pltpu.make_async_remote_copy(
            src_ref=msend.at[h], dst_ref=mrecv.at[r], send_sem=m_send.at[to], recv_sem=m_recv.at[r],
            device_id={"rep": to}, device_id_type=MESH,
        )

    def make(n, k):
        p = n * 4 + lax.rem(cell // 2 + k, 4)
        col = pl.multiple_of(p * 384, 128)
        first = wf[:, pl.ds(col, 128)]
        mid = wf[:, pl.ds(pl.multiple_of(col + 128, 128), 128)]
        last = wf[:, pl.ds(pl.multiple_of(col + 256, 128), 128)]
        mid_r = pltpu.roll(mid, DR, 1)
        last_r = pltpu.roll(last, DR, 1)
        pad = jnp.zeros((8, 128), F32)
        even = jnp.concatenate([jnp.where(low24, mid[:24], mid_r[24:]), pad], axis=0)
        odd = jnp.concatenate([jnp.where(low24, last_r[:24], last[24:]), pad], axis=0)
        msend[2 * p, 0:48] = first.astype(BF16)
        msend[2 * p, 48:64] = kf[:, pl.ds(pl.multiple_of(p * 256, 128), 128)].astype(BF16)
        msend[2 * p, 64:96] = even.astype(BF16)
        msend[2 * p + 1, 0:48] = jnp.where(low48, mid_r, last_r).astype(BF16)
        msend[2 * p + 1, 48:64] = kf[:, pl.ds(pl.multiple_of(p * 256 + 128, 128), 128)].astype(BF16)
        msend[2 * p + 1, 64:96] = odd.astype(BF16)
        for half in range(2):
            for g in range(2):
                to, copy = m_copy(2 * p + g, half)

                @pl.when(to != r)
                def _(copy=copy):
                    copy.start()

    def make_half(n):
        a_wait(1 + n)
        for k in range(XN):
            wf[12 * k : 12 * k + 12, 1536 * n : 1536 * n + 1536] = wx[k, :, 1536 * n : 1536 * n + 1536].astype(F32)

        def one(k, _):
            make(n, k)
            return 0

        lax.fori_loop(0, 4, one, 0)

    make_half(0)
    make_half(1)
    a_start(3)
    mrecv[r] = msend[head]

    def x_wait(k, _):
        frm = lax.rem(cell + k, 8)
        pltpu.make_async_remote_copy(
            src_ref=xsend, dst_ref=xrecv.at[frm, core], send_sem=x_send.at[k], recv_sem=x_recv.at[frm],
            device_id={"rep": base + 2 * frm + core}, device_id_type=MESH,
        ).wait_recv()
        return 0

    lax.fori_loop(1, 8, x_wait, 0)
    xc = pltpu.make_async_remote_copy(
        src_ref=xrecv.at[:, core], dst_ref=xrecv.at[:, core], send_sem=xc_sem.at[0], recv_sem=xc_sem.at[1],
        device_id={"rep": other}, device_id_type=MESH,
    )
    xc.start()

    a_wait(3)
    for k in range(XN):
        kf[4 * k : 4 * k + 4, :] = vx[k].astype(F32)
    vfull[zc, yc, core] = kf[...].astype(BF16)

    def v_peer(axis, k):
        if axis == 0:
            return lax.rem(zc + k, 4), yc
        return zc, lax.rem(yc + k, 4)

    def v_copy(hop, side, k):
        axis = side if hop == 0 else 1 - side
        to_z, to_y = v_peer(axis, k)
        cols = slice(1024 * side, 1024 * side + 1024)
        if hop == 0:
            block = vfull.at[zc, yc, core, :, cols]
        elif side == 0:
            block = vfull.at[:, yc, core, :, cols]
        else:
            block = vfull.at[zc, :, core, :, cols]
        return pltpu.make_async_remote_copy(
            src_ref=block, dst_ref=block, send_sem=v_send.at[hop, side, k],
            recv_sem=v_recv.at[hop, side, zc if axis == 0 else yc],
            device_id={"rep": to_z * 8 + to_y * 2 + core}, device_id_type=MESH,
        )

    def v_wait(hop, side, k):
        axis = side if hop == 0 else 1 - side
        from_z, from_y = v_peer(axis, k)
        cols = slice(1024 * side, 1024 * side + 1024)
        if hop == 0:
            block = vfull.at[from_z, from_y, core, :, cols]
        elif side == 0:
            block = vfull.at[:, from_y, core, :, cols]
        else:
            block = vfull.at[from_z, :, core, :, cols]
        pltpu.make_async_remote_copy(
            src_ref=block, dst_ref=block, send_sem=v_send.at[hop, side, k],
            recv_sem=v_recv.at[hop, side, from_z if axis == 0 else from_y],
            device_id={"rep": from_z * 8 + from_y * 2 + core}, device_id_type=MESH,
        ).wait_recv()

    def v_start(hop):
        for side in range(2):
            for k in (2, 1, 3):
                v_copy(hop, side, k).start()

    def v_wait_all(hop):
        for side in range(2):
            for k in (1, 3, 2):
                v_wait(hop, side, k)

    v_start(0)

    rope_copy.wait()

    def rope_step(a, _):
        top = pl.multiple_of(a * 32, 32)
        cat = jnp.concatenate(
            [
                jnp.concatenate(
                    [rope[pl.ds(top, 16), 128 * j : 128 * j + 128], rope[pl.ds(top + 16, 16), 128 * j : 128 * j + 128]],
                    axis=1,
                )
                for j in range(32)
            ],
            axis=0,
        )
        keep = (iota((256, 128), 1) < DR) == (lax.rem(iota((256, 128), 0), 2) == 0)
        for b in range(4):
            got = jnp.dot(pick[256 * b : 256 * b + 256, :], cat, preferred_element_type=F32)
            for g in range(2):
                v = got[:, 128 * g : 128 * g + 128]
                v = jnp.where(keep, v, pltpu.roll(v, DR, 1)).astype(BF16)
                zpool[pl.ds(a * 32 + g * 16 + b * 4, 4)] = v.reshape(4, 64, 128)
        return 0

    lax.fori_loop(0, POOL // 32, rope_step, 0)

    pltpu.make_async_remote_copy(
        src_ref=xrecv.at[:, 1 - core], dst_ref=xrecv.at[:, 1 - core], send_sem=xc_sem.at[0], recv_sem=xc_sem.at[1],
        device_id={"rep": other}, device_id_type=MESH,
    ).wait_recv()

    def spread(n, _):
        got = xrecv[n // 2, lax.rem(n, 2)]
        xexp[n, 0:16, :] = got[:, :QR]
        for j in range(4):
            mask = jnp.where(iota((16, TAIL), 0) // 4 == j, 1.0, 0.0).astype(BF16)
            xexp[n, 16:32, TAIL * j : TAIL * (j + 1)] = got[:, QR:] * mask
        return 0

    lax.fori_loop(0, GROUP, spread, 0)

    def m_wait(k, _):
        frm = lax.rem(r + k, REP)
        pltpu.make_async_remote_copy(
            src_ref=mrecv.at[frm], dst_ref=mrecv.at[frm], send_sem=m_send.at[k], recv_sem=m_recv.at[frm],
            device_id={"rep": frm}, device_id_type=MESH,
        ).wait_recv()
        return 0

    lax.fori_loop(1, REP, m_wait, 0)

    def place(j, _):
        block = mrecv[inv[j]]
        rows = pl.ds(pl.multiple_of(j * 48, 16), 48)
        wall[rows, 0:128] = block[0:48]
        t = block[64:96].astype(F32)[:24]
        t_r = pltpu.roll(t, DR, 1)
        low = iota((24, 128), 1) < DR
        both = jnp.concatenate([jnp.where(low, t, t_r), jnp.where(low, t_r, t)], axis=0)
        wall[rows, 128:256] = both.astype(BF16)
        return 0

    lax.fori_loop(0, REP, place, 0)

    key = mrecv[:, 48:64, :].reshape(LAT, 128)
    key = jnp.concatenate([key, key], axis=1)
    half = GROUP // 2

    qparts = ((qsend, qrecv), (qsend2, qrecv2))

    def q_copy(n, to):
        src, dst = qparts[n]
        return pltpu.make_async_remote_copy(
            src_ref=src.at[to], dst_ref=dst.at[head], send_sem=q_send.at[n, to], recv_sem=q_recv.at[n, mine],
            device_id={"rep": base + to}, device_id_type=MESH,
        )

    for e in (1, 0):
        group = pl.multiple_of(lax.rem(mine // half + e, 2) * half, half)
        members = pl.ds(group, half)
        raw = jnp.dot(xexp[members].reshape(half * 32, QR), wall[...], preferred_element_type=F32)
        raw = raw.reshape(half, 32, 256)
        tail = raw[:, 16:24] + raw[:, 24:32]
        tail = tail + jnp.concatenate([tail[:, 4:8], tail[:, 0:4]], axis=1)
        both = jnp.concatenate([raw[:, 0:16].reshape(half * 16, 256), tail.reshape(half * 8, 256)], axis=0)
        nope = both[:, :128]
        hi = nope.astype(BF16)
        lo = (nope - hi.astype(F32)).astype(BF16)
        lat = lax.dot_general(jnp.concatenate([hi, lo], axis=1), key, NT, preferred_element_type=F32)
        rot = both[:, 128:]
        rot_hi = rot.astype(BF16).astype(F32)
        rot = jnp.where(iota(rot.shape, 1) < DR, rot_hi, rot - rot_hi)
        nmain = half * 16
        lmain = lat[:nmain].reshape(half, 16, 512)
        rmain = rot[:nmain].reshape(half, 16, 128)
        ltail = lat[nmain:].reshape(half, 8, 512)
        rtail = rot[nmain:].reshape(half, 8, 128)
        first = lmain[:, 0:8]
        qsend[members, :, 0:256] = jnp.concatenate([first[:, :, :256], first[:, :, 256:]], axis=1).astype(BF16)
        qsend[members, :, 256:384] = jnp.concatenate([rmain[:, 0:8], rmain[:, 0:8]], axis=1).astype(BF16)

        def q_start(k, _, e=e, group=group):
            q_copy(0, group + lax.rem(mine + k, half)).start()
            return 0

        lax.fori_loop(1 - e, half, q_start, 0)
        second = lmain[:, 8:16]
        qsend2[members, :, 0:256] = jnp.concatenate([second[:, :, :256], second[:, :, 256:]], axis=1).astype(BF16)
        qsend2[members, :, 256:384] = jnp.concatenate([rmain[:, 8:16], rtail], axis=1).astype(BF16)
        upper = iota((half, 8, 128), 1) < 4
        pair = [
            jnp.where(upper, ltail[:, :, 256 * n : 256 * n + 128], ltail[:, :, 256 * n + 128 : 256 * n + 256])
            for n in range(2)
        ]
        qsend2[members, :, 384:512] = jnp.concatenate(pair, axis=1).astype(BF16)

    def q_start2(k, _):
        q_copy(1, lax.rem(mine + half + k, GROUP)).start()
        return 0

    lax.fori_loop(0, half, q_start2, 0)
    lax.fori_loop(half + 1, GROUP, q_start2, 0)
    qrecv[head] = qsend[mine]
    qrecv2[head] = qsend2[mine]

    v_wait_all(0)
    v_start(1)

    perm_row = iota((256, 256), 0)
    want = lax.rem(perm_row // 4, 16) * 16 + (perm_row // 64) * 4 + lax.rem(perm_row, 4)
    perm = jnp.where(iota((256, 256), 1) == want, 1.0, 0.0).astype(BF16)

    def q_wait_all(n):
        src, dst = qparts[n]

        def q_wait(k, _):
            frm = lax.rem(mine + k, GROUP)
            slot = lax.rem(frm, 2) * 8 + frm // 2
            pltpu.make_async_remote_copy(
                src_ref=src.at[frm], dst_ref=dst.at[slot], send_sem=q_send.at[n, frm], recv_sem=q_recv.at[n, frm],
                device_id={"rep": base + frm}, device_id_type=MESH,
            ).wait_recv()
            return 0

        lax.fori_loop(1, GROUP, q_wait, 0)

    low_q = iota((LAT, 128), 1) < DR
    low_r = iota((DR, 128), 1) < DR

    def stationary(i, lat_i, rp):
        rr = rp + pltpu.roll(rp, DR, 1)
        cos = jnp.concatenate([cs[i, 0]] * 8, axis=0)
        sin = jnp.concatenate([cs[i, 1]] * 8, axis=0)
        rr = rr * cos + pltpu.roll(rr, DR // 2, 1) * sin
        lat_t = jnp.transpose(jnp.concatenate([lat_i, lat_i], axis=0))
        rr_t = jnp.transpose(jnp.concatenate([rr, rr], axis=0))[:DR]
        left = jnp.where(low_q, lat_t, 0.0).astype(BF16)
        right = jnp.where(low_q, 0.0, lat_t).astype(BF16)
        rleft = jnp.where(low_r, rr_t, 0.0).astype(BF16)
        rright = jnp.where(low_r, 0.0, rr_t).astype(BF16)
        wqt[i, 0:512, 0:128] = left
        wqt[i, 512:1024, 0:128] = right
        wqt[i, 1024:1536, 128:256] = left
        wqt[i, 1536:2048, 128:256] = right
        wqt[i, 2048:2112, 0:128] = rleft
        wqt[i, 2112:2176, 0:128] = rright
        wqt[i, 2176:2240, 128:256] = rleft
        wqt[i, 2240:2304, 128:256] = rright

    def queries(n):
        q_wait_all(n)
        dst = qparts[n][1]
        got = jnp.dot(perm, dst[...].reshape(GROUP * 16, dst.shape[2]), preferred_element_type=F32)
        for m in range(2):
            left = got[64 * m : 64 * m + 64, :256]
            right = got[128 + 64 * m : 192 + 64 * m, :256]
            stationary(2 * n + m, jnp.concatenate([left, right], axis=1), got[64 * m : 64 * m + 64, 256:384])
        if n == 1:
            lat_i = jnp.concatenate([got[64 * j : 64 * j + 64, 384:512] for j in range(4)], axis=1)
            stationary(4, lat_i, got[128:192, 256:384])

    queries(0)
    pool_copy.wait()

    def page(i, c, k, g):
        return bt[i, c * 16 + k * 4 + g]

    def keys(i, c, k):
        return jnp.concatenate([pool[page(i, c, k, g)] for g in range(4)], axis=0)

    def scores(i, buf, slot, chunks):
        size = 256 * len(chunks)
        low = iota((64, 128), 1) < DR

        def latents(k):
            return jnp.concatenate([pool[page(i, c, k, g)] for c in chunks for g in range(4)], axis=0)

        def rotary(e):
            return jnp.concatenate(
                [
                    jnp.where(low, zpool[page(i, c, 2 * e, g)], zpool[page(i, c, 2 * e + 1, g)])
                    for c in chunks
                    for g in range(4)
                ],
                axis=0,
            )

        lhs = jnp.concatenate([latents(k) for k in range(4)] + [rotary(0), rotary(1)], axis=1)
        s = jnp.dot(lhs, wqt[i], preferred_element_type=F32)
        token = iota((256, 256), 0) + (iota((256, 256), 1) // 64) * 256
        m = m_sc[slot]
        for n, c in enumerate(chunks):
            part = jnp.where(token < ln[i] - c * 1024, s[256 * n : 256 * n + 256], NEG)
            buf[256 * c : 256 * c + 256, :] = part
            m = jnp.maximum(m, jnp.max(part.reshape(32, 8, 256), axis=0))
        m_sc[slot] = m

    def fresh(i, buf, slot):
        new = jnp.concatenate([nef[i], jnp.zeros((8, 640), F32)], axis=0).astype(BF16)
        s = jnp.dot(new[:, :LAT], wqt[i, 0:512], preferred_element_type=F32)
        s = s + jnp.dot(new[:, LAT:], wqt[i, 2048:2176], preferred_element_type=F32)
        u = iota((16, 256), 0)
        lane = iota((16, 256), 1)
        s = jnp.where((lane < 64) & (u <= lax.rem(lane, STEPS)), s, NEG)
        buf[1024:1040, :] = s
        m_sc[slot] = jnp.maximum(s[0:8], s[8:16])

    def top(slot):
        m = jnp.max(m_sc[slot], axis=0, keepdims=True)
        m = jnp.broadcast_to(m, (8, 256))
        m = jnp.maximum(m, pltpu.roll(m, 128, 1))
        m = jnp.maximum(m, pltpu.roll(m, 64, 1))
        return m

    def weigh(i, buf, slot):
        def chunk(c):
            s = buf[256 * c : 256 * c + 256, :]
            p = jnp.exp2((s - m_sc[slot][0:1]) * SCALE)
            l_sc[...] = l_sc[...] + jnp.sum(p.reshape(32, 8, 256), axis=0)
            pt = jnp.transpose(p).astype(BF16)
            t = acc[...]
            for k in range(4):
                t = t + jnp.dot(pt[64 * k : 64 * k + 64], keys(i, c, k), preferred_element_type=F32)
            acc[...] = t

        return chunk

    def weigh_fresh(i, buf, slot):
        s = buf[1024:1040, :]
        p = jnp.exp2((s - m_sc[slot][0:1]) * SCALE)
        l_sc[...] = p[0:8] + p[8:16]
        pt = jnp.transpose(jnp.concatenate([p[:, 0:128], jnp.zeros((112, 128), F32)], axis=0)).astype(BF16)
        new = jnp.concatenate([nef[i, :, :LAT], jnp.zeros((120, LAT), F32)], axis=0).astype(BF16)
        acc[...] = jnp.dot(pt[:64], new, preferred_element_type=F32)

    def finish(i):
        total = jnp.sum(l_sc[...], axis=0, keepdims=True)
        total = jnp.broadcast_to(total, (8, 256))
        total = total + pltpu.roll(total, 128, 1)
        total = total + pltpu.roll(total, 64, 1)
        col = jnp.transpose(jnp.broadcast_to(1.0 / total[0:1, :128], (128, 128)))[:64, 0:1]
        att[i] = acc[...] * col

    def forward():
        v_wait_all(1)
        pltpu.make_async_remote_copy(
            src_ref=vfull.at[:, :, core], dst_ref=vfull.at[:, :, core], send_sem=vc_sem.at[0], recv_sem=vc_sem.at[1],
            device_id={"rep": other}, device_id_type=MESH,
        ).start()

    bufs = (s_a, s_b)
    for i in range(REQ + 1):
        if i == 2:
            queries(1)
        if i < REQ:
            fresh(i, bufs[i % 2], i % 2)
        if i > 0:
            m_sc[(i - 1) % 2] = top((i - 1) % 2)
            weigh_fresh(i - 1, bufs[(i - 1) % 2], (i - 1) % 2)

        for c in range(0, 4, GATHER):
            if i < REQ:
                scores(i, bufs[i % 2], i % 2, list(range(c, c + GATHER)))
            if i > 0:
                for d in range(c, c + GATHER):
                    weigh(i - 1, bufs[(i - 1) % 2], (i - 1) % 2)(d)
        if i > 0:
            finish(i - 1)
        if i == 3:
            forward()

    pltpu.make_async_remote_copy(
        src_ref=vfull.at[:, :, 1 - core], dst_ref=vfull.at[:, :, 1 - core], send_sem=vc_sem.at[0], recv_sem=vc_sem.at[1],
        device_id={"rep": other}, device_id_type=MESH,
    ).wait_recv()
    for p in range(HEADS // 2):
        rows = att[:, 8 * p : 8 * p + 8, :].reshape(REQ * 8, LAT).astype(BF16)
        v = vfull[:, :, :, :, 256 * p : 256 * p + 256].reshape(LAT, 256)
        o = jnp.dot(rows, v, preferred_element_type=F32).reshape(REQ, 8, 256)
        for i in range(REQ):
            out_ref[i, :, 256 * p : 256 * p + 128] = o[i, 0:4, 0:128].astype(BF16)
            out_ref[i, :, 256 * p + 128 : 256 * p + 256] = o[i, 4:8, 128:256].astype(BF16)

    for n in range(4):
        for k in range(1, XN):
            a_copy(n, k).wait_send()

    def drain(k, _):
        x_copy(k).wait_send()
        return 0

    lax.fori_loop(1, 8, drain, 0)
    xc.wait_send()

    def drain_m(k, _):
        to = lax.rem(r + k, REP)
        m_copy(lax.rem(to, GROUP) // 2 + 8 * lax.rem(to, 2), to // GROUP)[1].wait_send()
        return 0

    lax.fori_loop(1, REP, drain_m, 0)

    def drain_q(k, _):
        q_copy(0, lax.rem(mine + k, GROUP)).wait_send()
        q_copy(1, lax.rem(mine + k, GROUP)).wait_send()
        return 0

    lax.fori_loop(1, GROUP, drain_q, 0)
    for hop in range(2):
        for side in range(2):
            for k in range(1, 4):
                v_copy(hop, side, k).wait_send()
    pltpu.make_async_remote_copy(
        src_ref=vfull.at[:, :, core], dst_ref=vfull.at[:, :, core], send_sem=vc_sem.at[0], recv_sem=vc_sem.at[1],
        device_id={"rep": other}, device_id_type=MESH,
    ).wait_send()


def on_device(query_latent, new_entry, cache_latent, cache_rope, block_table, context_len, owner_rows, query_up, key_up, value_up):
    half = DR // 2
    freq = np.float32(10000.0) ** (-np.arange(half, dtype=np.float32) / np.float32(half))
    freq = jnp.asarray(np.tile(freq, 4).reshape(1, 128).astype(np.float32))
    vmem = pl.BlockSpec(memory_space=pltpu.VMEM)
    smem = pl.BlockSpec(memory_space=pltpu.SMEM)
    hbm = pl.BlockSpec(memory_space=pl.ANY)
    dma = pltpu.SemaphoreType.DMA
    out = pl.pallas_call(
        kernel,
        out_shape=jax.ShapeDtypeStruct((REQ, STEPS, HEADS * DN), BF16),
        in_specs=[vmem, vmem, hbm, hbm, smem, smem, smem, hbm, hbm, hbm, vmem],
        out_specs=vmem,
        scratch_shapes=[
            pltpu.VMEM((POOL, 64, LAT), BF16),
            pltpu.VMEM((POOL, 64, 128), BF16),
            pltpu.VMEM((POOL, 4096), BF16),
            pltpu.VMEM((XN, 12, 3072), BF16),
            pltpu.VMEM((XN, 4, 2048), BF16),
            pltpu.VMEM((XN, 4, 2048), BF16),
            pltpu.VMEM((48, 3072), F32),
            pltpu.VMEM((16, 2048), F32),
            pltpu.VMEM((HEADS, MSG, 128), BF16),
            pltpu.VMEM((REP, MSG, 128), BF16),
            pltpu.VMEM((4, 4, 2, 16, 2048), BF16),
            pltpu.VMEM((16, XW), F32),
            pltpu.VMEM((16, XW), BF16),
            pltpu.VMEM((8, 2, 16, XW), BF16),
            pltpu.VMEM((GROUP, 32, QR), BF16),
            pltpu.VMEM((QR, 256), BF16),
            pltpu.VMEM((GROUP, 16, 384), BF16),
            pltpu.VMEM((GROUP, 16, 384), BF16),
            pltpu.VMEM((GROUP, 16, 512), BF16),
            pltpu.VMEM((GROUP, 16, 512), BF16),
            pltpu.VMEM((REQ, 2304, 256), BF16),
            pltpu.VMEM((1040, 256), F32),
            pltpu.VMEM((1040, 256), F32),
            pltpu.VMEM((2, 8, 256), F32),
            pltpu.VMEM((8, 256), F32),
            pltpu.VMEM((64, LAT), F32),
            pltpu.VMEM((REQ, 64, LAT), F32),
            pltpu.VMEM((REQ, 8, 640), F32),
            pltpu.VMEM((REQ, 2, 8, 128), F32),
            pltpu.VMEM((1024, 512), BF16),
            pltpu.SMEM((REP,), jnp.int32),
            dma((2,)), dma((4,)), dma((4, XN)), dma((4, XN)),
            dma((8,)), dma((8,)), dma((2,)), dma((REP,)), dma((REP,)),
            dma((2, 2, 4)), dma((2, 2, 4)), dma((2,)), dma((2, GROUP)), dma((2, GROUP)),
            pltpu.SemaphoreType.REGULAR, pltpu.SemaphoreType.REGULAR,
        ],
        compiler_params=pltpu.CompilerParams(
            collective_id=0, has_side_effects=True, vmem_limit_bytes=60 * 2**20
        ),
        name="latent_attention",
    )(jnp.swapaxes(query_latent, 0, 1), jnp.swapaxes(new_entry, 0, 1), cache_latent, cache_rope, block_table, context_len, owner_rows, query_up, key_up, value_up, freq)
    return jnp.swapaxes(out, 0, 1)


def solution(mesh):
    return jax.shard_map(
        on_device,
        mesh=mesh,
        in_specs=(
            P(None, "rep", None),
            P(None, "rep", None),
            P("rep", None, None),
            P("rep", None),
            P("rep", None),
            P("rep"),
            P(),
            P(("rep", "head"), None),
            P(("rep", "head"), None),
            P(("rep", "head"), None),
        ),
        out_specs=P(None, "rep", "head"),
        check_vma=False,
    )
```

```python
import functools

import jax
import jax.numpy as jnp
import numpy as np
from jax import lax
from jax.experimental import pallas as pl
from jax.experimental.pallas import tpu as pltpu
from jax.sharding import PartitionSpec as P

LAT = 512
DN = 128
DR = 64
STEPS = 4
REQ = 5
POOL = 320
QR = 1536
HEADS = 16
GROUP = 16
REP = 32
XN = 4
TAIL = QR // 4
XW = QR + TAIL
XCUT = 768
MSG = 96
SCALE = float((DN + DR) ** -0.5 * np.log2(np.e))
NEG = -1e30
GATHER = 2
MESH = pl.DeviceIdType.MESH
F32 = jnp.float32
BF16 = jnp.bfloat16
NT = (((1,), (1,)), ((), ()))


def iota(shape, dim):
    return lax.broadcasted_iota(jnp.int32, shape, dim)


def kernel(
    x_ref, ne_ref, lat_hbm, rope_hbm, bt, ln, own, wq_hbm, wk_hbm, wv_hbm, freq_ref, out_ref,
    pool, zpool, rope, wx, kx, vx, wf, kf, msend, mrecv, vfull, xs, xrecv, xexp, wall,
    qsend, qrecv, qsend2, qrecv2, wqt, s_a, s_b, m_sc, l_sc, acc, att, nef, cs, pick, inv,
    sem_local, sem_own, a_send, a_recv, x_send, x_recv, xc_sem, m_send, m_recv,
    v_send, v_recv, vc_sem, q_send, q_recv, row_sem, plane_sem,
):
    r = lax.axis_index("rep")
    hx = lax.axis_index("head")
    core = lax.rem(r, 2)
    zc = r // 8
    yc = lax.rem(r // 2, 4)
    base = (r // GROUP) * GROUP
    mine = lax.rem(r, GROUP)
    cell = mine // 2
    head = core * 8 + cell
    other = r + 1 - 2 * core

    rope_copy = pltpu.make_async_copy(rope_hbm, rope, sem_local.at[0])
    rope_copy.start()
    pool_copy = pltpu.make_async_copy(lat_hbm, pool, sem_local.at[1])
    pool_copy.start()

    def along(axis, k):
        if axis == "x":
            return {"head": lax.rem(hx + k, XN)}
        if axis == "core":
            return {"rep": other}
        if axis == "y":
            return {"rep": zc * 8 + lax.rem(yc + k, 4) * 2 + core}
        return {"rep": lax.rem(zc + k, 4) * 8 + yc * 2 + core}

    barrier = pltpu.get_barrier_semaphore()
    for axis in ("x", "core", "y", "z"):
        for k in range(1, 2 if axis == "core" else 4):
            pl.semaphore_signal(barrier, inc=1, device_id=along(axis, k), device_id_type=MESH)

    pl.semaphore_wait(barrier, 10)

    parts = (
        (wk_hbm, kx, 2048, 0, 2048),
        (wq_hbm, wx, 3072, 0, 1536),
        (wq_hbm, wx, 3072, 1536, 1536),
        (wv_hbm, vx, 2048, 0, 2048),
    )

    def a_source(n, to):
        src, dst, width, first, size = parts[n]
        return src.at[:, pl.ds(pl.multiple_of(to * width + first, 128), size)]

    def a_block(n, frm):
        src, dst, width, first, size = parts[n]
        return dst.at[frm, :, first : first + size]

    def a_copy(n, k):
        to = lax.rem(hx + k, XN)
        return pltpu.make_async_remote_copy(
            src_ref=a_source(n, to), dst_ref=a_block(n, hx), send_sem=a_send.at[n, k], recv_sem=a_recv.at[n, hx],
            device_id={"head": to}, device_id_type=MESH,
        )

    def a_wait(n):
        own_copy(n).wait()
        for k in range(1, XN):
            frm = lax.rem(hx + k, XN)
            pltpu.make_async_remote_copy(
                src_ref=a_block(n, frm), dst_ref=a_block(n, frm), send_sem=a_send.at[n, k], recv_sem=a_recv.at[n, frm],
                device_id={"head": frm}, device_id_type=MESH,
            ).wait_recv()

    def own_copy(n):
        return pltpu.make_async_copy(a_source(n, hx), a_block(n, hx), sem_own.at[n])

    def a_start(n):
        for k in (2, 1, 3):
            a_copy(n, k).start()
        own_copy(n).start()

    for n in range(3):
        a_start(n)
    for k in range(1, 4):
        pl.semaphore_signal(row_sem, inc=1, device_id=along("y", k), device_id_type=MESH)

    for i in range(4):
        xs[4 * i : 4 * i + 4, :QR] = x_ref[i].astype(F32)
    row = x_ref[4].astype(F32)
    for j in range(4):
        xs[4 * j : 4 * j + 4, QR:] = row[:, TAIL * j : TAIL * (j + 1)]

    zl = lax.rem(zc, 2)

    def x_cols(side):
        return slice(0, XCUT) if side == 0 else slice(XCUT, XW)

    def x_block(hop, side, zz, yy):
        if hop == 0:
            return xrecv.at[zz, yy, core, :, x_cols(side)]
        if side == 0:
            return xrecv.at[:, yy, core, :, x_cols(side)]
        return xrecv.at[zz, :, core, :, x_cols(side)]

    def x_move(hop, side, k, receive):
        zz, yy = zl, yc
        if (side == 0) == (hop == 0):
            zz = 1 - zl
            slot = 0
        else:
            yy = lax.rem(yc + k, 4)
            slot = yy if receive else yc
        block = x_block(hop, side, zz, yy) if receive else x_block(hop, side, zl, yc)
        return pltpu.make_async_remote_copy(
            src_ref=block, dst_ref=block, send_sem=x_send.at[hop, side, k], recv_sem=x_recv.at[hop, side, slot],
            device_id={"rep": (zc - zl + zz) * 8 + yy * 2 + core}, device_id_type=MESH,
        )

    def x_peers(hop, side):
        return (1,) if (side == 0) == (hop == 0) else (2, 1, 3)

    def x_all(hop, act):
        for side in (1, 0):
            for k in x_peers(hop, side):
                if act == "start":
                    x_move(hop, side, k, False).start()
                elif act == "wait":
                    x_move(hop, side, k, True).wait_recv()
                else:
                    x_move(hop, side, k, False).wait_send()

    xrecv[zl, yc, core] = xs[...].astype(BF16)
    x_all(0, "start")
    pl.semaphore_wait(row_sem, 3)
    for k in range(1, 4):
        pl.semaphore_signal(plane_sem, inc=1, device_id=along("z", k), device_id_type=MESH)

    def invert(j, _):
        at = jnp.int32(0)
        for n in range(REP):
            at = jnp.where(own[n] == j, jnp.int32(n), at)
        inv[j] = at
        return 0

    lax.fori_loop(0, REP, invert, 0)

    x_all(0, "wait")
    x_all(1, "start")

    lane8 = iota((8, 128), 1)
    sub8 = iota((8, 128), 0)
    sign = jnp.where(lax.rem(lane8, DR) < DR // 2, -1.0, 1.0).astype(F32)
    for i in range(REQ):
        angle = (ln[i] + lax.rem(sub8, STEPS)).astype(F32) * freq_ref[...]
        cs[i, 0] = jnp.cos(angle)
        cs[i, 1] = jnp.sin(angle) * sign
    nef[...] = jnp.zeros_like(nef)
    for i in range(REQ):
        nef[i, 0:STEPS, : LAT + DR] = ne_ref[i].astype(F32)
        v = nef[i, :, LAT:]
        v = v + pltpu.roll(v, DR, 1)
        v = v * cs[i, 0] + pltpu.roll(v, DR // 2, 1) * cs[i, 1]
        nef[i, :, LAT:] = jnp.where(lane8 < DR, v, 0.0)

    def clear(n, _):
        wqt[n // 9, pl.ds(pl.multiple_of(lax.rem(n, 9) * 256, 256), 256), :] = jnp.zeros((256, 256), BF16)
        return 0

    lax.fori_loop(0, REQ * 9, clear, 0)
    prow = iota((512, 256), 0)
    pcol = iota((512, 256), 1)
    pick[...] = jnp.where(
        (pcol // 16 == lax.rem(prow, 32) // 2) & (lax.rem(pcol, 16) == prow // 32), 1.0, 0.0
    ).astype(BF16)

    pl.semaphore_wait(plane_sem, 3)
    a_wait(0)
    for k in range(XN):
        kf[4 * k : 4 * k + 4, :] = kx[k].astype(F32)
    low48 = iota((48, 128), 1) < DR
    low24 = iota((24, 128), 1) < DR

    def m_copy(h, half):
        to = half * GROUP + lax.rem(h, 8) * 2 + h // 8
        return to, pltpu.make_async_remote_copy(
            src_ref=msend.at[h], dst_ref=mrecv.at[r], send_sem=m_send.at[0], recv_sem=m_recv.at[0],
            device_id={"rep": to}, device_id_type=MESH,
        )

    def make(n, k):
        p = n * 4 + lax.rem(cell // 2 + k, 4)
        col = pl.multiple_of(p * 384, 128)
        first = wf[:, pl.ds(col, 128)]
        mid = wf[:, pl.ds(pl.multiple_of(col + 128, 128), 128)]
        last = wf[:, pl.ds(pl.multiple_of(col + 256, 128), 128)]
        mid_r = pltpu.roll(mid, DR, 1)
        last_r = pltpu.roll(last, DR, 1)
        pad = jnp.zeros((8, 128), F32)
        even = jnp.concatenate([jnp.where(low24, mid[:24], mid_r[24:]), pad], axis=0)
        odd = jnp.concatenate([jnp.where(low24, last_r[:24], last[24:]), pad], axis=0)
        msend[2 * p, 0:48] = first.astype(BF16)
        msend[2 * p, 48:64] = kf[:, pl.ds(pl.multiple_of(p * 256, 128), 128)].astype(BF16)
        msend[2 * p, 64:96] = even.astype(BF16)
        msend[2 * p + 1, 0:48] = jnp.where(low48, mid_r, last_r).astype(BF16)
        msend[2 * p + 1, 48:64] = kf[:, pl.ds(pl.multiple_of(p * 256 + 128, 128), 128)].astype(BF16)
        msend[2 * p + 1, 64:96] = odd.astype(BF16)
        for half in range(2):
            for g in range(2):
                to, copy = m_copy(2 * p + g, half)

                @pl.when(to != r)
                def _(copy=copy):
                    copy.start()

    def make_half(n):
        a_wait(1 + n)
        for k in range(XN):
            wf[12 * k : 12 * k + 12, 1536 * n : 1536 * n + 1536] = wx[k, :, 1536 * n : 1536 * n + 1536].astype(F32)

        def one(k, _):
            make(n, k)
            return 0

        lax.fori_loop(0, 4, one, 0)

    make_half(0)
    make_half(1)
    a_start(3)
    mrecv[r] = msend[head]

    x_all(1, "wait")
    xc = pltpu.make_async_remote_copy(
        src_ref=xrecv.at[:, :, core], dst_ref=xrecv.at[:, :, core], send_sem=xc_sem.at[0], recv_sem=xc_sem.at[1],
        device_id={"rep": other}, device_id_type=MESH,
    )
    xc.start()

    a_wait(3)
    for k in range(XN):
        kf[4 * k : 4 * k + 4, :] = vx[k].astype(F32)
    vfull[zc, yc, core] = kf[...].astype(BF16)

    def v_peer(axis, k):
        if axis == 0:
            return lax.rem(zc + k, 4), yc
        return zc, lax.rem(yc + k, 4)

    def v_copy(hop, side, k):
        axis = side if hop == 0 else 1 - side
        to_z, to_y = v_peer(axis, k)
        cols = slice(1024 * side, 1024 * side + 1024)
        if hop == 0:
            block = vfull.at[zc, yc, core, :, cols]
        elif side == 0:
            block = vfull.at[:, yc, core, :, cols]
        else:
            block = vfull.at[zc, :, core, :, cols]
        return pltpu.make_async_remote_copy(
            src_ref=block, dst_ref=block, send_sem=v_send.at[hop, side, k],
            recv_sem=v_recv.at[hop, side, zc if axis == 0 else yc],
            device_id={"rep": to_z * 8 + to_y * 2 + core}, device_id_type=MESH,
        )

    def v_wait(hop, side, k):
        axis = side if hop == 0 else 1 - side
        from_z, from_y = v_peer(axis, k)
        cols = slice(1024 * side, 1024 * side + 1024)
        if hop == 0:
            block = vfull.at[from_z, from_y, core, :, cols]
        elif side == 0:
            block = vfull.at[:, from_y, core, :, cols]
        else:
            block = vfull.at[from_z, :, core, :, cols]
        pltpu.make_async_remote_copy(
            src_ref=block, dst_ref=block, send_sem=v_send.at[hop, side, k],
            recv_sem=v_recv.at[hop, side, from_z if axis == 0 else from_y],
            device_id={"rep": from_z * 8 + from_y * 2 + core}, device_id_type=MESH,
        ).wait_recv()

    def v_start(hop):
        for side in range(2):
            for k in (2, 1, 3):
                v_copy(hop, side, k).start()

    def v_wait_all(hop):
        for side in range(2):
            for k in (1, 3, 2):
                v_wait(hop, side, k)

    rope_copy.wait()

    def rope_step(a, _):
        top = pl.multiple_of(a * 32, 32)
        keep = (iota((512, 128), 1) < DR) == (lax.rem(iota((512, 128), 0), 2) == 0)
        for b in range(2):
            cat = jnp.concatenate(
                [
                    jnp.concatenate(
                        [
                            rope[pl.ds(top, 16), 128 * j : 128 * j + 128],
                            rope[pl.ds(top + 16, 16), 128 * j : 128 * j + 128],
                        ],
                        axis=1,
                    )
                    for j in range(16 * b, 16 * b + 16)
                ],
                axis=0,
            )
            got = jnp.dot(pick[...], cat, preferred_element_type=F32)
            for g in range(2):
                v = got[:, 128 * g : 128 * g + 128]
                v = jnp.where(keep, v, pltpu.roll(v, DR, 1)).astype(BF16)
                zpool[pl.ds(a * 32 + g * 16, 16), 32 * b : 32 * b + 32] = v.reshape(16, 32, 128)
        return 0

    lax.fori_loop(0, POOL // 32, rope_step, 0)

    pltpu.make_async_remote_copy(
        src_ref=xrecv.at[:, :, 1 - core], dst_ref=xrecv.at[:, :, 1 - core], send_sem=xc_sem.at[0], recv_sem=xc_sem.at[1],
        device_id={"rep": other}, device_id_type=MESH,
    ).wait_recv()

    masks = [jnp.where(iota((16, TAIL), 0) // 4 == j, 1.0, 0.0).astype(BF16) for j in range(4)]

    def spread(n, _):
        for d in range(4):
            got = xrecv[n // 2, 2 * lax.rem(n, 2) + d // 2, d % 2]
            xexp[4 * n + d, 0:16, :] = got[:, :QR]
            for j in range(4):
                xexp[4 * n + d, 16:32, TAIL * j : TAIL * (j + 1)] = got[:, QR:] * masks[j]
        return 0

    lax.fori_loop(0, GROUP // 4, spread, 0)

    def m_wait():
        block = mrecv.at[0 : REP - 1]
        return pltpu.make_async_remote_copy(
            src_ref=block, dst_ref=block, send_sem=m_send.at[0], recv_sem=m_recv.at[0],
            device_id={"rep": other}, device_id_type=MESH,
        )

    for n in range(4):
        for k in range(1, XN):
            a_copy(n, k).wait_send()
    x_all(0, "drain")
    x_all(1, "drain")
    m_wait().wait_recv()
    v_start(0)

    def place(n, _):
        low = iota((24, 128), 1) < DR
        for d in range(8):
            j = n * 8 + d
            block = mrecv[inv[j]]
            rows = pl.ds(pl.multiple_of(j * 48, 16), 48)
            wall[rows, 0:128] = block[0:48]
            t = block[64:96].astype(F32)[:24]
            t_r = pltpu.roll(t, DR, 1)
            both = jnp.concatenate([jnp.where(low, t, t_r), jnp.where(low, t_r, t)], axis=0)
            wall[rows, 128:256] = both.astype(BF16)
        return 0

    lax.fori_loop(0, REP // 8, place, 0)

    key = mrecv[:, 48:64, :].reshape(LAT, 128)
    key = jnp.concatenate([key, key], axis=1)
    half = GROUP // 2

    qparts = ((qsend, qrecv), (qsend2, qrecv2))

    def q_copy(n, to):
        src, dst = qparts[n]
        return pltpu.make_async_remote_copy(
            src_ref=src.at[to], dst_ref=dst.at[head], send_sem=q_send.at[n], recv_sem=q_recv.at[n],
            device_id={"rep": base + to}, device_id_type=MESH,
        )

    for e in (1, 0):
        group = pl.multiple_of(lax.rem(mine // half + e, 2) * half, half)
        members = pl.ds(group, half)
        raw = jnp.dot(xexp[members].reshape(half * 32, QR), wall[...], preferred_element_type=F32)
        raw = raw.reshape(half, 32, 256)
        tail = raw[:, 16:24] + raw[:, 24:32]
        tail = tail + jnp.concatenate([tail[:, 4:8], tail[:, 0:4]], axis=1)
        both = jnp.concatenate([raw[:, 0:16].reshape(half * 16, 256), tail.reshape(half * 8, 256)], axis=0)
        nope = both[:, :128]
        hi = nope.astype(BF16)
        lo = (nope - hi.astype(F32)).astype(BF16)
        lat = lax.dot_general(jnp.concatenate([hi, lo], axis=1), key, NT, preferred_element_type=F32)
        rot = both[:, 128:]
        rot_hi = rot.astype(BF16).astype(F32)
        rot = jnp.where(iota(rot.shape, 1) < DR, rot_hi, rot - rot_hi)
        nmain = half * 16
        lmain = lat[:nmain].reshape(half, 16, 512)
        rmain = rot[:nmain].reshape(half, 16, 128)
        ltail = lat[nmain:].reshape(half, 8, 512)
        rtail = rot[nmain:].reshape(half, 8, 128)
        first = lmain[:, 0:8]
        qsend[members, :, 0:256] = jnp.concatenate([first[:, :, :256], first[:, :, 256:]], axis=1).astype(BF16)
        qsend[members, :, 256:384] = jnp.concatenate([rmain[:, 0:8], rmain[:, 0:8]], axis=1).astype(BF16)

        def q_start(k, _, e=e, group=group):
            q_copy(0, group + lax.rem(mine + k, half)).start()
            return 0

        lax.fori_loop(1 - e, half, q_start, 0)
        second = lmain[:, 8:16]
        qsend2[members, :, 0:256] = jnp.concatenate([second[:, :, :256], second[:, :, 256:]], axis=1).astype(BF16)
        qsend2[members, :, 256:384] = jnp.concatenate([rmain[:, 8:16], rtail], axis=1).astype(BF16)
        upper = iota((half, 8, 128), 1) < 4
        pair = [
            jnp.where(upper, ltail[:, :, 256 * n : 256 * n + 128], ltail[:, :, 256 * n + 128 : 256 * n + 256])
            for n in range(2)
        ]
        qsend2[members, :, 384:512] = jnp.concatenate(pair, axis=1).astype(BF16)

    def q_start2(k, _):
        q_copy(1, lax.rem(mine + half + k, GROUP)).start()
        return 0

    lax.fori_loop(0, half, q_start2, 0)
    lax.fori_loop(half + 1, GROUP, q_start2, 0)
    qrecv[head] = qsend[mine]
    qrecv2[head] = qsend2[mine]

    xc.wait_send()
    m_wait().wait_send()
    perm_row = iota((256, 256), 0)
    want = lax.rem(perm_row // 4, 16) * 16 + (perm_row // 64) * 4 + lax.rem(perm_row, 4)
    perm = jnp.where(iota((256, 256), 1) == want, 1.0, 0.0).astype(BF16)

    def q_wait(n):
        block = qparts[n][1].at[0 : GROUP - 1]
        return pltpu.make_async_remote_copy(
            src_ref=block, dst_ref=block, send_sem=q_send.at[n], recv_sem=q_recv.at[n],
            device_id={"rep": other}, device_id_type=MESH,
        )

    low_q = iota((LAT, 128), 1) < DR
    low_r = iota((DR, 128), 1) < DR

    def stationary(i, lat_i, rp):
        rr = rp + pltpu.roll(rp, DR, 1)
        cos = jnp.concatenate([cs[i, 0]] * 8, axis=0)
        sin = jnp.concatenate([cs[i, 1]] * 8, axis=0)
        rr = rr * cos + pltpu.roll(rr, DR // 2, 1) * sin
        lat_t = jnp.transpose(jnp.concatenate([lat_i, lat_i], axis=0))
        rr_t = jnp.transpose(jnp.concatenate([rr, rr], axis=0))[:DR]
        left = jnp.where(low_q, lat_t, 0.0).astype(BF16)
        right = jnp.where(low_q, 0.0, lat_t).astype(BF16)
        rleft = jnp.where(low_r, rr_t, 0.0).astype(BF16)
        rright = jnp.where(low_r, 0.0, rr_t).astype(BF16)
        wqt[i, 0:512, 0:128] = left
        wqt[i, 512:1024, 0:128] = right
        wqt[i, 1024:1536, 128:256] = left
        wqt[i, 1536:2048, 128:256] = right
        wqt[i, 2048:2112, 0:128] = rleft
        wqt[i, 2112:2176, 0:128] = rright
        wqt[i, 2176:2240, 128:256] = rleft
        wqt[i, 2240:2304, 128:256] = rright

    def queries(n):
        q_wait(n).wait_recv()
        dst = qparts[n][1]
        got = jnp.dot(perm, dst[...].reshape(GROUP * 16, dst.shape[2]), preferred_element_type=F32)
        for m in range(2):
            left = got[64 * m : 64 * m + 64, :256]
            right = got[128 + 64 * m : 192 + 64 * m, :256]
            stationary(2 * n + m, jnp.concatenate([left, right], axis=1), got[64 * m : 64 * m + 64, 256:384])
        if n == 1:
            lat_i = jnp.concatenate([got[64 * j : 64 * j + 64, 384:512] for j in range(4)], axis=1)
            stationary(4, lat_i, got[128:192, 256:384])

    queries(0)
    v_wait_all(0)
    v_start(1)
    pool_copy.wait()

    def page(i, c, k, g):
        return bt[i, c * 16 + k * 4 + g]

    def keys(i, c, k):
        return jnp.concatenate([pool[page(i, c, k, g)] for g in range(4)], axis=0)

    def scores(i, buf, slot, chunks):
        size = 256 * len(chunks)
        low = iota((64, 128), 1) < DR

        def latents(k):
            return jnp.concatenate([pool[page(i, c, k, g)] for c in chunks for g in range(4)], axis=0)

        def rotary(e):
            return jnp.concatenate(
                [
                    jnp.where(low, zpool[page(i, c, 2 * e, g)], zpool[page(i, c, 2 * e + 1, g)])
                    for c in chunks
                    for g in range(4)
                ],
                axis=0,
            )

        lhs = jnp.concatenate([latents(k) for k in range(4)] + [rotary(0), rotary(1)], axis=1)
        s = jnp.dot(lhs, wqt[i], preferred_element_type=F32)
        token = iota((256, 256), 0) + (iota((256, 256), 1) // 64) * 256
        m = m_sc[slot]
        for n, c in enumerate(chunks):
            part = jnp.where(token < ln[i] - c * 1024, s[256 * n : 256 * n + 256], NEG)
            buf[256 * c : 256 * c + 256, :] = part
            m = jnp.maximum(m, jnp.max(part.reshape(32, 8, 256), axis=0))
        m_sc[slot] = m

    def fresh(i, buf, slot):
        new = jnp.concatenate([nef[i], jnp.zeros((8, 640), F32)], axis=0).astype(BF16)
        s = jnp.dot(new[:, :LAT], wqt[i, 0:512], preferred_element_type=F32)
        s = s + jnp.dot(new[:, LAT:], wqt[i, 2048:2176], preferred_element_type=F32)
        u = iota((16, 256), 0)
        lane = iota((16, 256), 1)
        s = jnp.where((lane < 64) & (u <= lax.rem(lane, STEPS)), s, NEG)
        buf[1024:1040, :] = s
        m_sc[slot] = jnp.maximum(s[0:8], s[8:16])

    def top(slot):
        m = jnp.max(m_sc[slot], axis=0, keepdims=True)
        m = jnp.broadcast_to(m, (8, 256))
        m = jnp.maximum(m, pltpu.roll(m, 128, 1))
        m = jnp.maximum(m, pltpu.roll(m, 64, 1))
        return m

    def weigh(i, buf, slot):
        def chunk(c):
            s = buf[256 * c : 256 * c + 256, :]
            p = jnp.exp2((s - m_sc[slot][0:1]) * SCALE)
            l_sc[...] = l_sc[...] + jnp.sum(p.reshape(32, 8, 256), axis=0)
            pt = jnp.transpose(p).astype(BF16)
            t = acc[...]
            for k in range(4):
                t = t + jnp.dot(pt[64 * k : 64 * k + 64], keys(i, c, k), preferred_element_type=F32)
            acc[...] = t

        return chunk

    def weigh_fresh(i, buf, slot):
        s = buf[1024:1040, :]
        p = jnp.exp2((s - m_sc[slot][0:1]) * SCALE)
        l_sc[...] = p[0:8] + p[8:16]
        pt = jnp.transpose(jnp.concatenate([p[:, 0:128], jnp.zeros((112, 128), F32)], axis=0)).astype(BF16)
        new = jnp.concatenate([nef[i, :, :LAT], jnp.zeros((120, LAT), F32)], axis=0).astype(BF16)
        acc[...] = jnp.dot(pt[:64], new, preferred_element_type=F32)

    def finish(i):
        total = jnp.sum(l_sc[...], axis=0, keepdims=True)
        total = jnp.broadcast_to(total, (8, 256))
        total = total + pltpu.roll(total, 128, 1)
        total = total + pltpu.roll(total, 64, 1)
        col = jnp.transpose(jnp.broadcast_to(1.0 / total[0:1, :128], (128, 128)))[:64, 0:1]
        att[i] = acc[...] * col

    def forward():
        v_wait_all(1)
        pltpu.make_async_remote_copy(
            src_ref=vfull.at[:, :, core], dst_ref=vfull.at[:, :, core], send_sem=vc_sem.at[0], recv_sem=vc_sem.at[1],
            device_id={"rep": other}, device_id_type=MESH,
        ).start()

    bufs = (s_a, s_b)
    for i in range(REQ + 1):
        if i == 2:
            queries(1)
        if i < REQ:
            fresh(i, bufs[i % 2], i % 2)
        if i > 0:
            m_sc[(i - 1) % 2] = top((i - 1) % 2)
            weigh_fresh(i - 1, bufs[(i - 1) % 2], (i - 1) % 2)

        for c in range(0, 4, GATHER):
            if i < REQ:
                scores(i, bufs[i % 2], i % 2, list(range(c, c + GATHER)))
            if i > 0:
                for d in range(c, c + GATHER):
                    weigh(i - 1, bufs[(i - 1) % 2], (i - 1) % 2)(d)
        if i > 0:
            finish(i - 1)
        if i == 3:
            forward()

    q_wait(0).wait_send()
    q_wait(1).wait_send()

    pltpu.make_async_remote_copy(
        src_ref=vfull.at[:, :, 1 - core], dst_ref=vfull.at[:, :, 1 - core], send_sem=vc_sem.at[0], recv_sem=vc_sem.at[1],
        device_id={"rep": other}, device_id_type=MESH,
    ).wait_recv()
    for p in range(HEADS // 2):
        rows = att[:, 8 * p : 8 * p + 8, :].reshape(REQ * 8, LAT).astype(BF16)
        v = vfull[:, :, :, :, 256 * p : 256 * p + 256].reshape(LAT, 256)
        o = jnp.dot(rows, v, preferred_element_type=F32).reshape(REQ, 8, 256)
        for i in range(REQ):
            out_ref[i, :, 256 * p : 256 * p + 128] = o[i, 0:4, 0:128].astype(BF16)
            out_ref[i, :, 256 * p + 128 : 256 * p + 256] = o[i, 4:8, 128:256].astype(BF16)

    for hop in range(2):
        for side in range(2):
            for k in range(1, 4):
                v_copy(hop, side, k).wait_send()
    pltpu.make_async_remote_copy(
        src_ref=vfull.at[:, :, core], dst_ref=vfull.at[:, :, core], send_sem=vc_sem.at[0], recv_sem=vc_sem.at[1],
        device_id={"rep": other}, device_id_type=MESH,
    ).wait_send()


def on_device(query_latent, new_entry, cache_latent, cache_rope, block_table, context_len, owner_rows, query_up, key_up, value_up):
    half = DR // 2
    freq = np.float32(10000.0) ** (-np.arange(half, dtype=np.float32) / np.float32(half))
    freq = jnp.asarray(np.tile(freq, 4).reshape(1, 128).astype(np.float32))
    vmem = pl.BlockSpec(memory_space=pltpu.VMEM)
    smem = pl.BlockSpec(memory_space=pltpu.SMEM)
    hbm = pl.BlockSpec(memory_space=pl.ANY)
    dma = pltpu.SemaphoreType.DMA
    out = pl.pallas_call(
        kernel,
        out_shape=jax.ShapeDtypeStruct((REQ, STEPS, HEADS * DN), BF16),
        in_specs=[vmem, vmem, hbm, hbm, smem, smem, smem, hbm, hbm, hbm, vmem],
        out_specs=vmem,
        scratch_shapes=[
            pltpu.VMEM((POOL, 64, LAT), BF16),
            pltpu.VMEM((POOL, 64, 128), BF16),
            pltpu.VMEM((POOL, 4096), BF16),
            pltpu.VMEM((XN, 12, 3072), BF16),
            pltpu.VMEM((XN, 4, 2048), BF16),
            pltpu.VMEM((XN, 4, 2048), BF16),
            pltpu.VMEM((48, 3072), F32),
            pltpu.VMEM((16, 2048), F32),
            pltpu.VMEM((HEADS, MSG, 128), BF16),
            pltpu.VMEM((REP, MSG, 128), BF16),
            pltpu.VMEM((4, 4, 2, 16, 2048), BF16),
            pltpu.VMEM((16, XW), F32),
            pltpu.VMEM((2, 4, 2, 16, XW), BF16),
            pltpu.VMEM((GROUP, 32, QR), BF16),
            pltpu.VMEM((QR, 256), BF16),
            pltpu.VMEM((GROUP, 16, 384), BF16),
            pltpu.VMEM((GROUP, 16, 384), BF16),
            pltpu.VMEM((GROUP, 16, 512), BF16),
            pltpu.VMEM((GROUP, 16, 512), BF16),
            pltpu.VMEM((REQ, 2304, 256), BF16),
            pltpu.VMEM((1040, 256), F32),
            pltpu.VMEM((1040, 256), F32),
            pltpu.VMEM((2, 8, 256), F32),
            pltpu.VMEM((8, 256), F32),
            pltpu.VMEM((64, LAT), F32),
            pltpu.VMEM((REQ, 64, LAT), F32),
            pltpu.VMEM((REQ, 8, 640), F32),
            pltpu.VMEM((REQ, 2, 8, 128), F32),
            pltpu.VMEM((512, 256), BF16),
            pltpu.SMEM((REP,), jnp.int32),
            dma((2,)), dma((4,)), dma((4, XN)), dma((4, XN)),
            dma((2, 2, 4)), dma((2, 2, 4)), dma((2,)), dma((1,)), dma((1,)),
            dma((2, 2, 4)), dma((2, 2, 4)), dma((2,)), dma((2,)), dma((2,)),
            pltpu.SemaphoreType.REGULAR, pltpu.SemaphoreType.REGULAR,
        ],
        compiler_params=pltpu.CompilerParams(
            collective_id=0, has_side_effects=True, vmem_limit_bytes=60 * 2**20
        ),
        name="latent_attention",
    )(jnp.swapaxes(query_latent, 0, 1), jnp.swapaxes(new_entry, 0, 1), cache_latent, cache_rope, block_table, context_len, owner_rows, query_up, key_up, value_up, freq)
    return jnp.swapaxes(out, 0, 1)


def solution(mesh):
    return jax.shard_map(
        on_device,
        mesh=mesh,
        in_specs=(
            P(None, "rep", None),
            P(None, "rep", None),
            P("rep", None, None),
            P("rep", None),
            P("rep", None),
            P("rep"),
            P(),
            P(("rep", "head"), None),
            P(("rep", "head"), None),
            P(("rep", "head"), None),
        ),
        out_specs=P(None, "rep", "head"),
        check_vma=False,
    )
```

```python
import functools

import jax
import jax.numpy as jnp
import numpy as np
from jax import lax
from jax.experimental import pallas as pl
from jax.experimental.pallas import tpu as pltpu
from jax.sharding import PartitionSpec as P

LAT = 512
DN = 128
DR = 64
STEPS = 4
REQ = 5
POOL = 320
QR = 1536
HEADS = 16
GROUP = 16
REP = 32
XN = 4
TAIL = QR // 4
XW = QR + TAIL
XCUT = 768
MSG = 88
SCALE = float((DN + DR) ** -0.5 * np.log2(np.e))
NEG = -1e30
GATHER = 2
MESH = pl.DeviceIdType.MESH
F32 = jnp.float32
BF16 = jnp.bfloat16
NT = (((1,), (1,)), ((), ()))


def iota(shape, dim):
    return lax.broadcasted_iota(jnp.int32, shape, dim)


def kernel(
    x_ref, ne_ref, lat_hbm, rope_hbm, bt, ln, own, wq_hbm, wk_hbm, wv_hbm, freq_ref, out_ref,
    pool, zpool, rope, wx, kx, vx, wf, kf, msend, mrecv, vfull, xs, xrecv, xexp, wall,
    qsend, qrecv, qsend2, qrecv2, wqt, s_a, s_b, m_sc, l_sc, acc, att, nef, cs, pick, inv,
    sem_local, sem_own, a_send, a_recv, x_send, x_recv, xc_sem, m_send, m_recv,
    v_send, v_recv, vc_sem, q_send, q_recv, row_sem, plane_sem,
):
    r = lax.axis_index("rep")
    hx = lax.axis_index("head")
    core = lax.rem(r, 2)
    zc = r // 8
    yc = lax.rem(r // 2, 4)
    base = (r // GROUP) * GROUP
    mine = lax.rem(r, GROUP)
    cell = mine // 2
    head = core * 8 + cell
    other = r + 1 - 2 * core

    rope_copy = pltpu.make_async_copy(rope_hbm, rope, sem_local.at[0])
    rope_copy.start()
    pool_copy = pltpu.make_async_copy(lat_hbm, pool, sem_local.at[1])
    pool_copy.start()

    def along(axis, k):
        if axis == "x":
            return {"head": lax.rem(hx + k, XN)}
        if axis == "core":
            return {"rep": other}
        if axis == "y":
            return {"rep": zc * 8 + lax.rem(yc + k, 4) * 2 + core}
        return {"rep": lax.rem(zc + k, 4) * 8 + yc * 2 + core}

    barrier = pltpu.get_barrier_semaphore()
    for axis in ("x", "core", "y", "z"):
        for k in range(1, 2 if axis == "core" else 4):
            pl.semaphore_signal(barrier, inc=1, device_id=along(axis, k), device_id_type=MESH)

    pl.semaphore_wait(barrier, 10)

    parts = (
        (wk_hbm, kx, 2048, 0, 2048),
        (wq_hbm, wx, 3072, 0, 1536),
        (wq_hbm, wx, 3072, 1536, 1536),
        (wv_hbm, vx, 2048, 0, 2048),
    )

    def a_source(n, to):
        src, dst, width, first, size = parts[n]
        return src.at[:, pl.ds(pl.multiple_of(to * width + first, 128), size)]

    def a_block(n, frm):
        src, dst, width, first, size = parts[n]
        return dst.at[frm, :, first : first + size]

    def a_copy(n, k):
        to = lax.rem(hx + k, XN)
        return pltpu.make_async_remote_copy(
            src_ref=a_source(n, to), dst_ref=a_block(n, hx), send_sem=a_send.at[n, k], recv_sem=a_recv.at[n, hx],
            device_id={"head": to}, device_id_type=MESH,
        )

    def a_wait(n):
        own_copy(n).wait()
        for k in range(1, XN):
            frm = lax.rem(hx + k, XN)
            pltpu.make_async_remote_copy(
                src_ref=a_block(n, frm), dst_ref=a_block(n, frm), send_sem=a_send.at[n, k], recv_sem=a_recv.at[n, frm],
                device_id={"head": frm}, device_id_type=MESH,
            ).wait_recv()

    def own_copy(n):
        return pltpu.make_async_copy(a_source(n, hx), a_block(n, hx), sem_own.at[n])

    def a_start(n):
        for k in (2, 1, 3):
            a_copy(n, k).start()
        own_copy(n).start()

    for n in range(3):
        a_start(n)
    for k in range(1, 4):
        pl.semaphore_signal(row_sem, inc=1, device_id=along("y", k), device_id_type=MESH)

    for i in range(4):
        xs[4 * i : 4 * i + 4, :QR] = x_ref[i].astype(F32)
    row = x_ref[4].astype(F32)
    for j in range(4):
        xs[4 * j : 4 * j + 4, QR:] = row[:, TAIL * j : TAIL * (j + 1)]

    zl = lax.rem(zc, 2)

    def x_cols(side):
        return slice(0, XCUT) if side == 0 else slice(XCUT, XW)

    def x_block(hop, side, zz, yy):
        if hop == 0:
            return xrecv.at[zz, yy, core, :, x_cols(side)]
        if side == 0:
            return xrecv.at[:, yy, core, :, x_cols(side)]
        return xrecv.at[zz, :, core, :, x_cols(side)]

    def x_move(hop, side, k, receive):
        zz, yy = zl, yc
        if (side == 0) == (hop == 0):
            zz = 1 - zl
            slot = 0
        else:
            yy = lax.rem(yc + k, 4)
            slot = yy if receive else yc
        block = x_block(hop, side, zz, yy) if receive else x_block(hop, side, zl, yc)
        return pltpu.make_async_remote_copy(
            src_ref=block, dst_ref=block, send_sem=x_send.at[hop, side, k], recv_sem=x_recv.at[hop, side, slot],
            device_id={"rep": (zc - zl + zz) * 8 + yy * 2 + core}, device_id_type=MESH,
        )

    def x_peers(hop, side):
        return (1,) if (side == 0) == (hop == 0) else (2, 1, 3)

    def x_all(hop, act):
        for side in (1, 0):
            for k in x_peers(hop, side):
                if act == "start":
                    x_move(hop, side, k, False).start()
                elif act == "wait":
                    x_move(hop, side, k, True).wait_recv()
                else:
                    x_move(hop, side, k, False).wait_send()

    xrecv[zl, yc, core] = xs[...].astype(BF16)
    x_all(0, "start")
    pl.semaphore_wait(row_sem, 3)
    for k in range(1, 4):
        pl.semaphore_signal(plane_sem, inc=1, device_id=along("z", k), device_id_type=MESH)

    def invert(j, _):
        at = jnp.int32(0)
        for n in range(REP):
            at = jnp.where(own[n] == j, jnp.int32(n), at)
        inv[j] = at
        return 0

    lax.fori_loop(0, REP, invert, 0)

    x_all(0, "wait")
    x_all(1, "start")

    lane8 = iota((8, 128), 1)
    sub8 = iota((8, 128), 0)
    sign = jnp.where(lax.rem(lane8, DR) < DR // 2, -1.0, 1.0).astype(F32)
    for i in range(REQ):
        angle = (ln[i] + lax.rem(sub8, STEPS)).astype(F32) * freq_ref[...]
        cs[i, 0] = jnp.cos(angle)
        cs[i, 1] = jnp.sin(angle) * sign
    nef[...] = jnp.zeros_like(nef)
    for i in range(REQ):
        nef[i, 0:STEPS, : LAT + DR] = ne_ref[i].astype(F32)
        v = nef[i, :, LAT:]
        v = v + pltpu.roll(v, DR, 1)
        v = v * cs[i, 0] + pltpu.roll(v, DR // 2, 1) * cs[i, 1]
        nef[i, :, LAT:] = jnp.where(lane8 < DR, v, 0.0)

    def clear(n, _):
        wqt[n // 9, pl.ds(pl.multiple_of(lax.rem(n, 9) * 256, 256), 256), :] = jnp.zeros((256, 256), BF16)
        return 0

    lax.fori_loop(0, REQ * 9, clear, 0)
    prow = iota((512, 256), 0)
    pcol = iota((512, 256), 1)
    pick[...] = jnp.where(
        (pcol // 16 == lax.rem(prow, 32) // 2) & (lax.rem(pcol, 16) == prow // 32), 1.0, 0.0
    ).astype(BF16)

    pl.semaphore_wait(plane_sem, 3)
    a_wait(0)
    for k in range(XN):
        kf[4 * k : 4 * k + 4, :] = kx[k].astype(F32)
    low48 = iota((48, 128), 1) < DR
    low24 = iota((24, 128), 1) < DR

    def m_copy(h, half):
        to = half * GROUP + lax.rem(h, 8) * 2 + h // 8
        return to, pltpu.make_async_remote_copy(
            src_ref=msend.at[h], dst_ref=mrecv.at[r], send_sem=m_send.at[0], recv_sem=m_recv.at[0],
            device_id={"rep": to}, device_id_type=MESH,
        )

    def make(n, k):
        p = n * 4 + lax.rem(cell // 2 + k, 4)
        col = pl.multiple_of(p * 384, 128)
        first = wf[:, pl.ds(col, 128)]
        mid = wf[:, pl.ds(pl.multiple_of(col + 128, 128), 128)]
        last = wf[:, pl.ds(pl.multiple_of(col + 256, 128), 128)]
        mid_r = pltpu.roll(mid, DR, 1)
        last_r = pltpu.roll(last, DR, 1)
        even = jnp.where(low24, mid[:24], mid_r[24:])
        odd = jnp.where(low24, last_r[:24], last[24:])
        msend[2 * p, 0:48] = first.astype(BF16)
        msend[2 * p, 48:64] = kf[:, pl.ds(pl.multiple_of(p * 256, 128), 128)].astype(BF16)
        msend[2 * p, 64:88] = even.astype(BF16)
        msend[2 * p + 1, 0:48] = jnp.where(low48, mid_r, last_r).astype(BF16)
        msend[2 * p + 1, 48:64] = kf[:, pl.ds(pl.multiple_of(p * 256 + 128, 128), 128)].astype(BF16)
        msend[2 * p + 1, 64:88] = odd.astype(BF16)
        for half in range(2):
            for g in range(2):
                to, copy = m_copy(2 * p + g, half)

                @pl.when(to != r)
                def _(copy=copy):
                    copy.start()

    def make_half(n):
        a_wait(1 + n)
        for k in range(XN):
            wf[12 * k : 12 * k + 12, 1536 * n : 1536 * n + 1536] = wx[k, :, 1536 * n : 1536 * n + 1536].astype(F32)

        def one(k, _):
            make(n, k)
            return 0

        lax.fori_loop(0, 4, one, 0)

    make_half(0)
    make_half(1)
    a_start(3)
    mrecv[r] = msend[head]

    x_all(1, "wait")
    xc = pltpu.make_async_remote_copy(
        src_ref=xrecv.at[:, :, core], dst_ref=xrecv.at[:, :, core], send_sem=xc_sem.at[0], recv_sem=xc_sem.at[1],
        device_id={"rep": other}, device_id_type=MESH,
    )
    xc.start()

    a_wait(3)
    for k in range(XN):
        kf[4 * k : 4 * k + 4, :] = vx[k].astype(F32)
    vfull[zc, yc, core] = kf[...].astype(BF16)

    def v_peer(axis, k):
        if axis == 0:
            return lax.rem(zc + k, 4), yc
        return zc, lax.rem(yc + k, 4)

    def v_copy(hop, side, k):
        axis = side if hop == 0 else 1 - side
        to_z, to_y = v_peer(axis, k)
        cols = slice(1024 * side, 1024 * side + 1024)
        if hop == 0:
            block = vfull.at[zc, yc, core, :, cols]
        elif side == 0:
            block = vfull.at[:, yc, core, :, cols]
        else:
            block = vfull.at[zc, :, core, :, cols]
        return pltpu.make_async_remote_copy(
            src_ref=block, dst_ref=block, send_sem=v_send.at[hop, side, k],
            recv_sem=v_recv.at[hop, side, zc if axis == 0 else yc],
            device_id={"rep": to_z * 8 + to_y * 2 + core}, device_id_type=MESH,
        )

    def v_wait(hop, side, k):
        axis = side if hop == 0 else 1 - side
        from_z, from_y = v_peer(axis, k)
        cols = slice(1024 * side, 1024 * side + 1024)
        if hop == 0:
            block = vfull.at[from_z, from_y, core, :, cols]
        elif side == 0:
            block = vfull.at[:, from_y, core, :, cols]
        else:
            block = vfull.at[from_z, :, core, :, cols]
        pltpu.make_async_remote_copy(
            src_ref=block, dst_ref=block, send_sem=v_send.at[hop, side, k],
            recv_sem=v_recv.at[hop, side, from_z if axis == 0 else from_y],
            device_id={"rep": from_z * 8 + from_y * 2 + core}, device_id_type=MESH,
        ).wait_recv()

    def v_start(hop):
        for side in range(2):
            for k in (2, 1, 3):
                v_copy(hop, side, k).start()

    def v_wait_all(hop):
        for side in range(2):
            for k in (1, 3, 2):
                v_wait(hop, side, k)

    rope_copy.wait()

    def rope_step(a, _):
        top = pl.multiple_of(a * 32, 32)
        keep = (iota((512, 128), 1) < DR) == (lax.rem(iota((512, 128), 0), 2) == 0)
        for b in range(2):
            cat = jnp.concatenate(
                [
                    jnp.concatenate(
                        [
                            rope[pl.ds(top, 16), 128 * j : 128 * j + 128],
                            rope[pl.ds(top + 16, 16), 128 * j : 128 * j + 128],
                        ],
                        axis=1,
                    )
                    for j in range(16 * b, 16 * b + 16)
                ],
                axis=0,
            )
            got = jnp.dot(pick[...], cat, preferred_element_type=F32)
            for g in range(2):
                v = got[:, 128 * g : 128 * g + 128]
                v = jnp.where(keep, v, pltpu.roll(v, DR, 1)).astype(BF16)
                zpool[pl.ds(a * 32 + g * 16, 16), 32 * b : 32 * b + 32] = v.reshape(16, 32, 128)
        return 0

    lax.fori_loop(0, POOL // 32, rope_step, 0)

    pltpu.make_async_remote_copy(
        src_ref=xrecv.at[:, :, 1 - core], dst_ref=xrecv.at[:, :, 1 - core], send_sem=xc_sem.at[0], recv_sem=xc_sem.at[1],
        device_id={"rep": other}, device_id_type=MESH,
    ).wait_recv()

    masks = [jnp.where(iota((16, TAIL), 0) // 4 == j, 1.0, 0.0).astype(BF16) for j in range(4)]

    def spread(n, _):
        for d in range(4):
            got = xrecv[n // 2, 2 * lax.rem(n, 2) + d // 2, d % 2]
            xexp[4 * n + d, 0:16, :] = got[:, :QR]
            for j in range(4):
                xexp[4 * n + d, 16:32, TAIL * j : TAIL * (j + 1)] = got[:, QR:] * masks[j]
        return 0

    lax.fori_loop(0, GROUP // 4, spread, 0)

    def m_wait():
        block = mrecv.at[0 : REP - 1]
        return pltpu.make_async_remote_copy(
            src_ref=block, dst_ref=block, send_sem=m_send.at[0], recv_sem=m_recv.at[0],
            device_id={"rep": other}, device_id_type=MESH,
        )

    for n in range(4):
        for k in range(1, XN):
            a_copy(n, k).wait_send()
    x_all(0, "drain")
    x_all(1, "drain")
    m_wait().wait_recv()
    v_start(0)

    def place(n, _):
        low = iota((24, 128), 1) < DR
        for d in range(8):
            j = n * 8 + d
            block = mrecv[inv[j]]
            rows = pl.ds(pl.multiple_of(j * 48, 16), 48)
            wall[rows, 0:128] = block[0:48]
            t = block[64:88].astype(F32)
            t_r = pltpu.roll(t, DR, 1)
            both = jnp.concatenate([jnp.where(low, t, t_r), jnp.where(low, t_r, t)], axis=0)
            wall[rows, 128:256] = both.astype(BF16)
        return 0

    lax.fori_loop(0, REP // 8, place, 0)

    key = mrecv[:, 48:64, :].reshape(LAT, 128)
    key = jnp.concatenate([key, key], axis=1)
    half = GROUP // 2

    qparts = ((qsend, qrecv), (qsend2, qrecv2))

    def q_copy(n, to):
        src, dst = qparts[n]
        return pltpu.make_async_remote_copy(
            src_ref=src.at[to], dst_ref=dst.at[head], send_sem=q_send.at[n], recv_sem=q_recv.at[n],
            device_id={"rep": base + to}, device_id_type=MESH,
        )

    for e in (1, 0):
        group = pl.multiple_of(lax.rem(mine // half + e, 2) * half, half)
        members = pl.ds(group, half)
        raw = jnp.dot(xexp[members].reshape(half * 32, QR), wall[...], preferred_element_type=F32)
        raw = raw.reshape(half, 32, 256)
        tail = raw[:, 16:24] + raw[:, 24:32]
        tail = tail + jnp.concatenate([tail[:, 4:8], tail[:, 0:4]], axis=1)
        both = jnp.concatenate([raw[:, 0:16].reshape(half * 16, 256), tail.reshape(half * 8, 256)], axis=0)
        nope = both[:, :128]
        hi = nope.astype(BF16)
        lo = (nope - hi.astype(F32)).astype(BF16)
        lat = lax.dot_general(jnp.concatenate([hi, lo], axis=1), key, NT, preferred_element_type=F32)
        rot = both[:, 128:]
        rot_hi = rot.astype(BF16).astype(F32)
        rot = jnp.where(iota(rot.shape, 1) < DR, rot_hi, rot - rot_hi)
        nmain = half * 16
        lmain = lat[:nmain].reshape(half, 16, 512)
        rmain = rot[:nmain].reshape(half, 16, 128)
        ltail = lat[nmain:].reshape(half, 8, 512)
        rtail = rot[nmain:].reshape(half, 8, 128)
        first = lmain[:, 0:8]
        qsend[members, :, 0:256] = jnp.concatenate([first[:, :, :256], first[:, :, 256:]], axis=1).astype(BF16)
        qsend[members, :, 256:384] = jnp.concatenate([rmain[:, 0:8], rmain[:, 0:8]], axis=1).astype(BF16)

        def q_start(k, _, e=e, group=group):
            q_copy(0, group + lax.rem(mine + k, half)).start()
            return 0

        lax.fori_loop(1 - e, half, q_start, 0)
        second = lmain[:, 8:16]
        qsend2[members, :, 0:256] = jnp.concatenate([second[:, :, :256], second[:, :, 256:]], axis=1).astype(BF16)
        qsend2[members, :, 256:384] = jnp.concatenate([rmain[:, 8:16], rtail], axis=1).astype(BF16)
        upper = iota((half, 8, 128), 1) < 4
        pair = [
            jnp.where(upper, ltail[:, :, 256 * n : 256 * n + 128], ltail[:, :, 256 * n + 128 : 256 * n + 256])
            for n in range(2)
        ]
        qsend2[members, :, 384:512] = jnp.concatenate(pair, axis=1).astype(BF16)

    def q_start2(k, _):
        q_copy(1, lax.rem(mine + half + k, GROUP)).start()
        return 0

    lax.fori_loop(0, half, q_start2, 0)
    lax.fori_loop(half + 1, GROUP, q_start2, 0)
    qrecv[head] = qsend[mine]
    qrecv2[head] = qsend2[mine]

    xc.wait_send()
    m_wait().wait_send()
    perm_row = iota((256, 256), 0)
    want = lax.rem(perm_row // 4, 16) * 16 + (perm_row // 64) * 4 + lax.rem(perm_row, 4)
    perm = jnp.where(iota((256, 256), 1) == want, 1.0, 0.0).astype(BF16)

    def q_wait(n):
        block = qparts[n][1].at[0 : GROUP - 1]
        return pltpu.make_async_remote_copy(
            src_ref=block, dst_ref=block, send_sem=q_send.at[n], recv_sem=q_recv.at[n],
            device_id={"rep": other}, device_id_type=MESH,
        )

    low_q = iota((LAT, 128), 1) < DR
    low_r = iota((DR, 128), 1) < DR

    def stationary(i, lat_i, rp):
        rr = rp + pltpu.roll(rp, DR, 1)
        cos = jnp.concatenate([cs[i, 0]] * 8, axis=0)
        sin = jnp.concatenate([cs[i, 1]] * 8, axis=0)
        rr = rr * cos + pltpu.roll(rr, DR // 2, 1) * sin
        lat_t = jnp.transpose(jnp.concatenate([lat_i, lat_i], axis=0))
        rr_t = jnp.transpose(jnp.concatenate([rr, rr], axis=0))[:DR]
        left = jnp.where(low_q, lat_t, 0.0).astype(BF16)
        right = jnp.where(low_q, 0.0, lat_t).astype(BF16)
        rleft = jnp.where(low_r, rr_t, 0.0).astype(BF16)
        rright = jnp.where(low_r, 0.0, rr_t).astype(BF16)
        wqt[i, 0:512, 0:128] = left
        wqt[i, 512:1024, 0:128] = right
        wqt[i, 1024:1536, 128:256] = left
        wqt[i, 1536:2048, 128:256] = right
        wqt[i, 2048:2112, 0:128] = rleft
        wqt[i, 2112:2176, 0:128] = rright
        wqt[i, 2176:2240, 128:256] = rleft
        wqt[i, 2240:2304, 128:256] = rright

    def queries(n):
        q_wait(n).wait_recv()
        dst = qparts[n][1]
        got = jnp.dot(perm, dst[...].reshape(GROUP * 16, dst.shape[2]), preferred_element_type=F32)
        for m in range(2):
            left = got[64 * m : 64 * m + 64, :256]
            right = got[128 + 64 * m : 192 + 64 * m, :256]
            stationary(2 * n + m, jnp.concatenate([left, right], axis=1), got[64 * m : 64 * m + 64, 256:384])
        if n == 1:
            lat_i = jnp.concatenate([got[64 * j : 64 * j + 64, 384:512] for j in range(4)], axis=1)
            stationary(4, lat_i, got[128:192, 256:384])

    queries(0)
    v_wait_all(0)
    v_start(1)
    pool_copy.wait()

    def page(i, c, k, g):
        return bt[i, c * 16 + k * 4 + g]

    def keys(i, c, k):
        return jnp.concatenate([pool[page(i, c, k, g)] for g in range(4)], axis=0)

    def scores(i, buf, slot, chunks):
        size = 256 * len(chunks)
        low = iota((64, 128), 1) < DR

        def latents(k):
            return jnp.concatenate([pool[page(i, c, k, g)] for c in chunks for g in range(4)], axis=0)

        def rotary(e):
            return jnp.concatenate(
                [
                    jnp.where(low, zpool[page(i, c, 2 * e, g)], zpool[page(i, c, 2 * e + 1, g)])
                    for c in chunks
                    for g in range(4)
                ],
                axis=0,
            )

        lhs = jnp.concatenate([latents(k) for k in range(4)] + [rotary(0), rotary(1)], axis=1)
        s = jnp.dot(lhs, wqt[i], preferred_element_type=F32)
        token = iota((256, 256), 0) + (iota((256, 256), 1) // 64) * 256
        m = m_sc[slot]
        for n, c in enumerate(chunks):
            part = jnp.where(token < ln[i] - c * 1024, s[256 * n : 256 * n + 256], NEG)
            buf[256 * c : 256 * c + 256, :] = part
            m = jnp.maximum(m, jnp.max(part.reshape(32, 8, 256), axis=0))
        m_sc[slot] = m

    def fresh(i, buf, slot):
        new = jnp.concatenate([nef[i], jnp.zeros((8, 640), F32)], axis=0).astype(BF16)
        s = jnp.dot(new[:, :LAT], wqt[i, 0:512], preferred_element_type=F32)
        s = s + jnp.dot(new[:, LAT:], wqt[i, 2048:2176], preferred_element_type=F32)
        u = iota((16, 256), 0)
        lane = iota((16, 256), 1)
        s = jnp.where((lane < 64) & (u <= lax.rem(lane, STEPS)), s, NEG)
        buf[1024:1040, :] = s
        m_sc[slot] = jnp.maximum(s[0:8], s[8:16])

    def top(slot):
        m = jnp.max(m_sc[slot], axis=0, keepdims=True)
        m = jnp.broadcast_to(m, (8, 256))
        m = jnp.maximum(m, pltpu.roll(m, 128, 1))
        m = jnp.maximum(m, pltpu.roll(m, 64, 1))
        return m

    def weigh(i, buf, slot):
        def chunk(c):
            s = buf[256 * c : 256 * c + 256, :]
            p = jnp.exp2((s - m_sc[slot][0:1]) * SCALE)
            l_sc[...] = l_sc[...] + jnp.sum(p.reshape(32, 8, 256), axis=0)
            pt = jnp.transpose(p).astype(BF16)
            t = acc[...]
            for k in range(4):
                t = t + jnp.dot(pt[64 * k : 64 * k + 64], keys(i, c, k), preferred_element_type=F32)
            acc[...] = t

        return chunk

    def weigh_fresh(i, buf, slot):
        s = buf[1024:1040, :]
        p = jnp.exp2((s - m_sc[slot][0:1]) * SCALE)
        l_sc[...] = p[0:8] + p[8:16]
        pt = jnp.transpose(jnp.concatenate([p[:, 0:128], jnp.zeros((112, 128), F32)], axis=0)).astype(BF16)
        new = jnp.concatenate([nef[i, :, :LAT], jnp.zeros((120, LAT), F32)], axis=0).astype(BF16)
        acc[...] = jnp.dot(pt[:64], new, preferred_element_type=F32)

    def finish(i):
        total = jnp.sum(l_sc[...], axis=0, keepdims=True)
        total = jnp.broadcast_to(total, (8, 256))
        total = total + pltpu.roll(total, 128, 1)
        total = total + pltpu.roll(total, 64, 1)
        col = jnp.transpose(jnp.broadcast_to(1.0 / total[0:1, :128], (128, 128)))[:64, 0:1]
        att[i] = acc[...] * col

    def forward():
        v_wait_all(1)
        pltpu.make_async_remote_copy(
            src_ref=vfull.at[:, :, core], dst_ref=vfull.at[:, :, core], send_sem=vc_sem.at[0], recv_sem=vc_sem.at[1],
            device_id={"rep": other}, device_id_type=MESH,
        ).start()

    bufs = (s_a, s_b)
    for i in range(REQ + 1):
        if i == 2:
            queries(1)
        if i < REQ:
            fresh(i, bufs[i % 2], i % 2)
        if i > 0:
            m_sc[(i - 1) % 2] = top((i - 1) % 2)
            weigh_fresh(i - 1, bufs[(i - 1) % 2], (i - 1) % 2)

        for c in range(0, 4, GATHER):
            if i < REQ:
                scores(i, bufs[i % 2], i % 2, list(range(c, c + GATHER)))
            if i > 0:
                for d in range(c, c + GATHER):
                    weigh(i - 1, bufs[(i - 1) % 2], (i - 1) % 2)(d)
        if i > 0:
            finish(i - 1)
        if i == 3:
            forward()

    q_wait(0).wait_send()
    q_wait(1).wait_send()
    for hop in range(2):
        for side in range(2):
            for k in range(1, 4):
                v_copy(hop, side, k).wait_send()

    pltpu.make_async_remote_copy(
        src_ref=vfull.at[:, :, 1 - core], dst_ref=vfull.at[:, :, 1 - core], send_sem=vc_sem.at[0], recv_sem=vc_sem.at[1],
        device_id={"rep": other}, device_id_type=MESH,
    ).wait_recv()
    for p in range(HEADS // 2):
        rows = att[:, 8 * p : 8 * p + 8, :].reshape(REQ * 8, LAT).astype(BF16)
        v = vfull[:, :, :, :, 256 * p : 256 * p + 256].reshape(LAT, 256)
        o = jnp.dot(rows, v, preferred_element_type=F32).reshape(REQ, 8, 256)
        for i in range(REQ):
            out_ref[i, :, 256 * p : 256 * p + 128] = o[i, 0:4, 0:128].astype(BF16)
            out_ref[i, :, 256 * p + 128 : 256 * p + 256] = o[i, 4:8, 128:256].astype(BF16)

    pltpu.make_async_remote_copy(
        src_ref=vfull.at[:, :, core], dst_ref=vfull.at[:, :, core], send_sem=vc_sem.at[0], recv_sem=vc_sem.at[1],
        device_id={"rep": other}, device_id_type=MESH,
    ).wait_send()


def on_device(query_latent, new_entry, cache_latent, cache_rope, block_table, context_len, owner_rows, query_up, key_up, value_up):
    half = DR // 2
    freq = np.float32(10000.0) ** (-np.arange(half, dtype=np.float32) / np.float32(half))
    freq = jnp.asarray(np.tile(freq, 4).reshape(1, 128).astype(np.float32))
    vmem = pl.BlockSpec(memory_space=pltpu.VMEM)
    smem = pl.BlockSpec(memory_space=pltpu.SMEM)
    hbm = pl.BlockSpec(memory_space=pl.ANY)
    dma = pltpu.SemaphoreType.DMA
    out = pl.pallas_call(
        kernel,
        out_shape=jax.ShapeDtypeStruct((REQ, STEPS, HEADS * DN), BF16),
        in_specs=[vmem, vmem, hbm, hbm, smem, smem, smem, hbm, hbm, hbm, vmem],
        out_specs=vmem,
        scratch_shapes=[
            pltpu.VMEM((POOL, 64, LAT), BF16),
            pltpu.VMEM((POOL, 64, 128), BF16),
            pltpu.VMEM((POOL, 4096), BF16),
            pltpu.VMEM((XN, 12, 3072), BF16),
            pltpu.VMEM((XN, 4, 2048), BF16),
            pltpu.VMEM((XN, 4, 2048), BF16),
            pltpu.VMEM((48, 3072), F32),
            pltpu.VMEM((16, 2048), F32),
            pltpu.VMEM((HEADS, MSG, 128), BF16),
            pltpu.VMEM((REP, MSG, 128), BF16),
            pltpu.VMEM((4, 4, 2, 16, 2048), BF16),
            pltpu.VMEM((16, XW), F32),
            pltpu.VMEM((2, 4, 2, 16, XW), BF16),
            pltpu.VMEM((GROUP, 32, QR), BF16),
            pltpu.VMEM((QR, 256), BF16),
            pltpu.VMEM((GROUP, 16, 384), BF16),
            pltpu.VMEM((GROUP, 16, 384), BF16),
            pltpu.VMEM((GROUP, 16, 512), BF16),
            pltpu.VMEM((GROUP, 16, 512), BF16),
            pltpu.VMEM((REQ, 2304, 256), BF16),
            pltpu.VMEM((1040, 256), F32),
            pltpu.VMEM((1040, 256), F32),
            pltpu.VMEM((2, 8, 256), F32),
            pltpu.VMEM((8, 256), F32),
            pltpu.VMEM((64, LAT), F32),
            pltpu.VMEM((REQ, 64, LAT), F32),
            pltpu.VMEM((REQ, 8, 640), F32),
            pltpu.VMEM((REQ, 2, 8, 128), F32),
            pltpu.VMEM((512, 256), BF16),
            pltpu.SMEM((REP,), jnp.int32),
            dma((2,)), dma((4,)), dma((4, XN)), dma((4, XN)),
            dma((2, 2, 4)), dma((2, 2, 4)), dma((2,)), dma((1,)), dma((1,)),
            dma((2, 2, 4)), dma((2, 2, 4)), dma((2,)), dma((2,)), dma((2,)),
            pltpu.SemaphoreType.REGULAR, pltpu.SemaphoreType.REGULAR,
        ],
        compiler_params=pltpu.CompilerParams(
            collective_id=0, has_side_effects=True, vmem_limit_bytes=60 * 2**20
        ),
        name="latent_attention",
    )(jnp.swapaxes(query_latent, 0, 1), jnp.swapaxes(new_entry, 0, 1), cache_latent, cache_rope, block_table, context_len, owner_rows, query_up, key_up, value_up, freq)
    return jnp.swapaxes(out, 0, 1)


def solution(mesh):
    return jax.shard_map(
        on_device,
        mesh=mesh,
        in_specs=(
            P(None, "rep", None),
            P(None, "rep", None),
            P("rep", None, None),
            P("rep", None),
            P("rep", None),
            P("rep"),
            P(),
            P(("rep", "head"), None),
            P(("rep", "head"), None),
            P(("rep", "head"), None),
        ),
        out_specs=P(None, "rep", "head"),
        check_vma=False,
    )
```

```python
import functools

import jax
import jax.numpy as jnp
import numpy as np
from jax import lax
from jax.experimental import pallas as pl
from jax.experimental.pallas import tpu as pltpu
from jax.sharding import PartitionSpec as P

LAT = 512
DN = 128
DR = 64
STEPS = 4
REQ = 5
POOL = 320
QR = 1536
HEADS = 16
GROUP = 16
REP = 32
XN = 4
TAIL = QR // 4
XW = QR + TAIL
XCUT = 768
MSG = 88
SCALE = float((DN + DR) ** -0.5 * np.log2(np.e))
NEG = -1e30
GATHER = 2
MESH = pl.DeviceIdType.MESH
F32 = jnp.float32
BF16 = jnp.bfloat16
NT = (((1,), (1,)), ((), ()))


def iota(shape, dim):
    return lax.broadcasted_iota(jnp.int32, shape, dim)


def kernel(
    x_ref, ne_ref, lat_hbm, rope_hbm, bt, ln, own, wq_hbm, wk_hbm, wv_hbm, freq_ref, out_ref,
    pool, zpool, rope, wx, kx, vx, wf, kf, msend, mrecv, vfull, xs, xrecv, xexp, wall,
    qsend, qrecv, qsend2, qrecv2, wqt, s_a, s_b, m_sc, l_sc, acc, att, nef, cs, pick, inv,
    sem_local, sem_own, a_send, a_recv, x_send, x_recv, xc_sem, m_send, m_recv,
    v_send, v_recv, vc_sem, q_send, q_recv, row_sem, plane_sem,
):
    r = lax.axis_index("rep")
    hx = lax.axis_index("head")
    core = lax.rem(r, 2)
    zc = r // 8
    yc = lax.rem(r // 2, 4)
    base = (r // GROUP) * GROUP
    mine = lax.rem(r, GROUP)
    cell = mine // 2
    head = core * 8 + cell
    other = r + 1 - 2 * core

    rope_copy = pltpu.make_async_copy(rope_hbm, rope, sem_local.at[0])
    rope_copy.start()
    pool_copy = pltpu.make_async_copy(lat_hbm, pool, sem_local.at[1])
    pool_copy.start()

    def along(axis, k):
        if axis == "x":
            return {"head": lax.rem(hx + k, XN)}
        if axis == "core":
            return {"rep": other}
        if axis == "y":
            return {"rep": zc * 8 + lax.rem(yc + k, 4) * 2 + core}
        return {"rep": lax.rem(zc + k, 4) * 8 + yc * 2 + core}

    barrier = pltpu.get_barrier_semaphore()
    for axis in ("x", "core", "y", "z"):
        for k in range(1, 2 if axis == "core" else 4):
            pl.semaphore_signal(barrier, inc=1, device_id=along(axis, k), device_id_type=MESH)

    pl.semaphore_wait(barrier, 10)

    parts = (
        (wk_hbm, kx, 2048, 0, 2048),
        (wq_hbm, wx, 3072, 0, 1536),
        (wq_hbm, wx, 3072, 1536, 1536),
        (wv_hbm, vx, 2048, 0, 2048),
    )

    def a_source(n, to):
        src, dst, width, first, size = parts[n]
        return src.at[:, pl.ds(pl.multiple_of(to * width + first, 128), size)]

    def a_block(n, frm):
        src, dst, width, first, size = parts[n]
        return dst.at[frm, :, first : first + size]

    def a_copy(n, k):
        to = lax.rem(hx + k, XN)
        return pltpu.make_async_remote_copy(
            src_ref=a_source(n, to), dst_ref=a_block(n, hx), send_sem=a_send.at[n, k], recv_sem=a_recv.at[n, hx],
            device_id={"head": to}, device_id_type=MESH,
        )

    def a_wait(n):
        own_copy(n).wait()
        for k in range(1, XN):
            frm = lax.rem(hx + k, XN)
            pltpu.make_async_remote_copy(
                src_ref=a_block(n, frm), dst_ref=a_block(n, frm), send_sem=a_send.at[n, k], recv_sem=a_recv.at[n, frm],
                device_id={"head": frm}, device_id_type=MESH,
            ).wait_recv()

    def own_copy(n):
        return pltpu.make_async_copy(a_source(n, hx), a_block(n, hx), sem_own.at[n])

    def a_start(n):
        for k in (2, 1, 3):
            a_copy(n, k).start()
        own_copy(n).start()

    for n in range(3):
        a_start(n)
    for k in range(1, 4):
        pl.semaphore_signal(row_sem, inc=1, device_id=along("y", k), device_id_type=MESH)

    for i in range(4):
        xs[4 * i : 4 * i + 4, :QR] = x_ref[i].astype(F32)
    row = x_ref[4].astype(F32)
    for j in range(4):
        xs[4 * j : 4 * j + 4, QR:] = row[:, TAIL * j : TAIL * (j + 1)]

    zl = lax.rem(zc, 2)

    def x_cols(side):
        return slice(0, XCUT) if side == 0 else slice(XCUT, XW)

    def x_block(hop, side, zz, yy):
        if hop == 0:
            return xrecv.at[zz, yy, core, :, x_cols(side)]
        if side == 0:
            return xrecv.at[:, yy, core, :, x_cols(side)]
        return xrecv.at[zz, :, core, :, x_cols(side)]

    def x_move(hop, side, k, receive):
        zz, yy = zl, yc
        if (side == 0) == (hop == 0):
            zz = 1 - zl
            slot = 0
        else:
            yy = lax.rem(yc + k, 4)
            slot = yy if receive else yc
        block = x_block(hop, side, zz, yy) if receive else x_block(hop, side, zl, yc)
        return pltpu.make_async_remote_copy(
            src_ref=block, dst_ref=block, send_sem=x_send.at[hop, side, k], recv_sem=x_recv.at[hop, side, slot],
            device_id={"rep": (zc - zl + zz) * 8 + yy * 2 + core}, device_id_type=MESH,
        )

    def x_peers(hop, side):
        return (1,) if (side == 0) == (hop == 0) else (2, 1, 3)

    def x_all(hop, act):
        for side in (1, 0):
            for k in x_peers(hop, side):
                if act == "start":
                    x_move(hop, side, k, False).start()
                elif act == "wait":
                    x_move(hop, side, k, True).wait_recv()
                else:
                    x_move(hop, side, k, False).wait_send()

    xrecv[zl, yc, core] = xs[...].astype(BF16)
    x_all(0, "start")
    pl.semaphore_wait(row_sem, 3)
    for k in range(1, 4):
        pl.semaphore_signal(plane_sem, inc=1, device_id=along("z", k), device_id_type=MESH)

    def invert(j, _):
        at = jnp.int32(0)
        for n in range(REP):
            at = jnp.where(own[n] == j, jnp.int32(n), at)
        inv[j] = at
        return 0

    lax.fori_loop(0, REP, invert, 0)

    x_all(0, "wait")
    x_all(1, "start")

    lane8 = iota((8, 128), 1)
    sub8 = iota((8, 128), 0)
    sign = jnp.where(lax.rem(lane8, DR) < DR // 2, -1.0, 1.0).astype(F32)
    for i in range(REQ):
        angle = (ln[i] + lax.rem(sub8, STEPS)).astype(F32) * freq_ref[...]
        cs[i, 0] = jnp.cos(angle)
        cs[i, 1] = jnp.sin(angle) * sign
    nef[...] = jnp.zeros_like(nef)
    for i in range(REQ):
        nef[i, 0:STEPS, : LAT + DR] = ne_ref[i].astype(F32)
        v = nef[i, :, LAT:]
        v = v + pltpu.roll(v, DR, 1)
        v = v * cs[i, 0] + pltpu.roll(v, DR // 2, 1) * cs[i, 1]
        nef[i, :, LAT:] = jnp.where(lane8 < DR, v, 0.0)

    def clear(n, _):
        wqt[n // 9, pl.ds(pl.multiple_of(lax.rem(n, 9) * 256, 256), 256), :] = jnp.zeros((256, 256), BF16)
        return 0

    lax.fori_loop(0, REQ * 9, clear, 0)
    prow = iota((512, 256), 0)
    pcol = iota((512, 256), 1)
    pick[...] = jnp.where(
        (pcol // 16 == lax.rem(prow, 32) // 2) & (lax.rem(pcol, 16) == prow // 32), 1.0, 0.0
    ).astype(BF16)

    pl.semaphore_wait(plane_sem, 3)
    a_wait(0)
    for k in range(XN):
        kf[4 * k : 4 * k + 4, :] = kx[k].astype(F32)
    low48 = iota((48, 128), 1) < DR
    low24 = iota((24, 128), 1) < DR

    def m_copy(h, half):
        to = half * GROUP + lax.rem(h, 8) * 2 + h // 8
        return to, pltpu.make_async_remote_copy(
            src_ref=msend.at[h], dst_ref=mrecv.at[r], send_sem=m_send.at[0], recv_sem=m_recv.at[0],
            device_id={"rep": to}, device_id_type=MESH,
        )

    def make(n, k):
        p = n * 4 + lax.rem(cell // 2 + k, 4)
        col = pl.multiple_of(p * 384, 128)
        first = wf[:, pl.ds(col, 128)]
        mid = wf[:, pl.ds(pl.multiple_of(col + 128, 128), 128)]
        last = wf[:, pl.ds(pl.multiple_of(col + 256, 128), 128)]
        mid_r = pltpu.roll(mid, DR, 1)
        last_r = pltpu.roll(last, DR, 1)
        even = jnp.where(low24, mid[:24], mid_r[24:])
        odd = jnp.where(low24, last_r[:24], last[24:])
        msend[2 * p, 0:48] = first.astype(BF16)
        msend[2 * p, 48:64] = kf[:, pl.ds(pl.multiple_of(p * 256, 128), 128)].astype(BF16)
        msend[2 * p, 64:88] = even.astype(BF16)
        msend[2 * p + 1, 0:48] = jnp.where(low48, mid_r, last_r).astype(BF16)
        msend[2 * p + 1, 48:64] = kf[:, pl.ds(pl.multiple_of(p * 256 + 128, 128), 128)].astype(BF16)
        msend[2 * p + 1, 64:88] = odd.astype(BF16)
        for half in range(2):
            for g in range(2):
                to, copy = m_copy(2 * p + g, half)

                @pl.when(to != r)
                def _(copy=copy):
                    copy.start()

    def make_half(n):
        a_wait(1 + n)
        for k in range(XN):
            wf[12 * k : 12 * k + 12, 1536 * n : 1536 * n + 1536] = wx[k, :, 1536 * n : 1536 * n + 1536].astype(F32)

        def one(k, _):
            make(n, k)
            return 0

        lax.fori_loop(0, 4, one, 0)

    make_half(0)
    make_half(1)
    a_start(3)
    mrecv[r] = msend[head]

    x_all(1, "wait")
    xc = pltpu.make_async_remote_copy(
        src_ref=xrecv.at[:, :, core], dst_ref=xrecv.at[:, :, core], send_sem=xc_sem.at[0], recv_sem=xc_sem.at[1],
        device_id={"rep": other}, device_id_type=MESH,
    )
    xc.start()

    a_wait(3)
    for k in range(XN):
        kf[4 * k : 4 * k + 4, :] = vx[k].astype(F32)
    vfull[zc, yc, core] = kf[...].astype(BF16)

    def v_peer(axis, k):
        if axis == 0:
            return lax.rem(zc + k, 4), yc
        return zc, lax.rem(yc + k, 4)

    def v_copy(hop, side, k):
        axis = side if hop == 0 else 1 - side
        to_z, to_y = v_peer(axis, k)
        cols = slice(1024 * side, 1024 * side + 1024)
        if hop == 0:
            block = vfull.at[zc, yc, core, :, cols]
        elif side == 0:
            block = vfull.at[:, yc, core, :, cols]
        else:
            block = vfull.at[zc, :, core, :, cols]
        return pltpu.make_async_remote_copy(
            src_ref=block, dst_ref=block, send_sem=v_send.at[hop, side, k],
            recv_sem=v_recv.at[hop, side, zc if axis == 0 else yc],
            device_id={"rep": to_z * 8 + to_y * 2 + core}, device_id_type=MESH,
        )

    def v_wait(hop, side, k):
        axis = side if hop == 0 else 1 - side
        from_z, from_y = v_peer(axis, k)
        cols = slice(1024 * side, 1024 * side + 1024)
        if hop == 0:
            block = vfull.at[from_z, from_y, core, :, cols]
        elif side == 0:
            block = vfull.at[:, from_y, core, :, cols]
        else:
            block = vfull.at[from_z, :, core, :, cols]
        pltpu.make_async_remote_copy(
            src_ref=block, dst_ref=block, send_sem=v_send.at[hop, side, k],
            recv_sem=v_recv.at[hop, side, from_z if axis == 0 else from_y],
            device_id={"rep": from_z * 8 + from_y * 2 + core}, device_id_type=MESH,
        ).wait_recv()

    def v_start(hop):
        for side in range(2):
            for k in (2, 1, 3):
                v_copy(hop, side, k).start()

    def v_wait_all(hop):
        for side in range(2):
            for k in (1, 3, 2):
                v_wait(hop, side, k)

    rope_copy.wait()

    def rope_step(a, _):
        top = pl.multiple_of(a * 32, 32)
        keep = (iota((512, 128), 1) < DR) == (lax.rem(iota((512, 128), 0), 2) == 0)
        for b in range(2):
            cat = jnp.concatenate(
                [
                    jnp.concatenate(
                        [
                            rope[pl.ds(top, 16), 128 * j : 128 * j + 128],
                            rope[pl.ds(top + 16, 16), 128 * j : 128 * j + 128],
                        ],
                        axis=1,
                    )
                    for j in range(16 * b, 16 * b + 16)
                ],
                axis=0,
            )
            got = jnp.dot(pick[...], cat, preferred_element_type=F32)
            for g in range(2):
                v = got[:, 128 * g : 128 * g + 128]
                v = jnp.where(keep, v, pltpu.roll(v, DR, 1)).astype(BF16)
                zpool[pl.ds(a * 32 + g * 16, 16), 32 * b : 32 * b + 32] = v.reshape(16, 32, 128)
        return 0

    lax.fori_loop(0, POOL // 32, rope_step, 0)

    pltpu.make_async_remote_copy(
        src_ref=xrecv.at[:, :, 1 - core], dst_ref=xrecv.at[:, :, 1 - core], send_sem=xc_sem.at[0], recv_sem=xc_sem.at[1],
        device_id={"rep": other}, device_id_type=MESH,
    ).wait_recv()

    masks = [jnp.where(iota((16, TAIL), 0) // 4 == j, 1.0, 0.0).astype(BF16) for j in range(4)]

    def spread(n, _):
        for d in range(4):
            got = xrecv[n // 2, 2 * lax.rem(n, 2) + d // 2, d % 2]
            xexp[4 * n + d, 0:16, :] = got[:, :QR]
            for j in range(4):
                xexp[4 * n + d, 16:32, TAIL * j : TAIL * (j + 1)] = got[:, QR:] * masks[j]
        return 0

    lax.fori_loop(0, GROUP // 4, spread, 0)

    def m_wait():
        block = mrecv.at[0 : REP - 1]
        return pltpu.make_async_remote_copy(
            src_ref=block, dst_ref=block, send_sem=m_send.at[0], recv_sem=m_recv.at[0],
            device_id={"rep": other}, device_id_type=MESH,
        )

    for n in range(4):
        for k in range(1, XN):
            a_copy(n, k).wait_send()
    x_all(0, "drain")
    x_all(1, "drain")
    m_wait().wait_recv()
    v_start(0)

    def place(n, _):
        low = iota((24, 128), 1) < DR
        for d in range(8):
            j = n * 8 + d
            block = mrecv[inv[j]]
            rows = pl.ds(pl.multiple_of(j * 48, 16), 48)
            wall[rows, 0:128] = block[0:48]
            t = block[64:88].astype(F32)
            t_r = pltpu.roll(t, DR, 1)
            both = jnp.concatenate([jnp.where(low, t, t_r), jnp.where(low, t_r, t)], axis=0)
            wall[rows, 128:256] = both.astype(BF16)
        return 0

    lax.fori_loop(0, REP // 8, place, 0)

    key = mrecv[:, 48:64, :].reshape(LAT, 128)
    key = jnp.concatenate([key, key], axis=1)
    half = GROUP // 2

    qparts = ((qsend, qrecv), (qsend2, qrecv2))

    def q_copy(n, to):
        src, dst = qparts[n]
        return pltpu.make_async_remote_copy(
            src_ref=src.at[to], dst_ref=dst.at[head], send_sem=q_send.at[n], recv_sem=q_recv.at[n],
            device_id={"rep": base + to}, device_id_type=MESH,
        )

    for e in (1, 0):
        group = pl.multiple_of(lax.rem(mine // half + e, 2) * half, half)
        members = pl.ds(group, half)
        raw = jnp.dot(xexp[members].reshape(half * 32, QR), wall[...], preferred_element_type=F32)
        raw = raw.reshape(half, 32, 256)
        tail = raw[:, 16:24] + raw[:, 24:32]
        tail = tail + jnp.concatenate([tail[:, 4:8], tail[:, 0:4]], axis=1)
        both = jnp.concatenate([raw[:, 0:16].reshape(half * 16, 256), tail.reshape(half * 8, 256)], axis=0)
        nope = both[:, :128]
        hi = nope.astype(BF16)
        lo = (nope - hi.astype(F32)).astype(BF16)
        lat = lax.dot_general(jnp.concatenate([hi, lo], axis=1), key, NT, preferred_element_type=F32)
        rot = both[:, 128:]
        rot_hi = rot.astype(BF16).astype(F32)
        rot = jnp.where(iota(rot.shape, 1) < DR, rot_hi, rot - rot_hi)
        nmain = half * 16
        lmain = lat[:nmain].reshape(half, 16, 512)
        rmain = rot[:nmain].reshape(half, 16, 128)
        ltail = lat[nmain:].reshape(half, 8, 512)
        rtail = rot[nmain:].reshape(half, 8, 128)
        first = lmain[:, 0:8]
        qsend[members, :, 0:256] = jnp.concatenate([first[:, :, :256], first[:, :, 256:]], axis=1).astype(BF16)
        qsend[members, :, 256:384] = jnp.concatenate([rmain[:, 0:8], rmain[:, 0:8]], axis=1).astype(BF16)

        def q_start(k, _, e=e, group=group):
            q_copy(0, group + lax.rem(mine + k, half)).start()
            return 0

        lax.fori_loop(1 - e, half, q_start, 0)
        second = lmain[:, 8:16]
        qsend2[members, :, 0:256] = jnp.concatenate([second[:, :, :256], second[:, :, 256:]], axis=1).astype(BF16)
        qsend2[members, :, 256:384] = jnp.concatenate([rmain[:, 8:16], rtail], axis=1).astype(BF16)
        upper = iota((half, 8, 128), 1) < 4
        pair = [
            jnp.where(upper, ltail[:, :, 256 * n : 256 * n + 128], ltail[:, :, 256 * n + 128 : 256 * n + 256])
            for n in range(2)
        ]
        qsend2[members, :, 384:512] = jnp.concatenate(pair, axis=1).astype(BF16)

    def q_start2(k, _):
        q_copy(1, lax.rem(mine + half + k, GROUP)).start()
        return 0

    lax.fori_loop(0, half, q_start2, 0)
    lax.fori_loop(half + 1, GROUP, q_start2, 0)
    qrecv[head] = qsend[mine]
    qrecv2[head] = qsend2[mine]

    xc.wait_send()
    m_wait().wait_send()
    perm_row = iota((256, 256), 0)
    want = lax.rem(perm_row // 4, 16) * 16 + (perm_row // 64) * 4 + lax.rem(perm_row, 4)
    perm = jnp.where(iota((256, 256), 1) == want, 1.0, 0.0).astype(BF16)

    def q_wait(n):
        block = qparts[n][1].at[0 : GROUP - 1]
        return pltpu.make_async_remote_copy(
            src_ref=block, dst_ref=block, send_sem=q_send.at[n], recv_sem=q_recv.at[n],
            device_id={"rep": other}, device_id_type=MESH,
        )

    low_q = iota((LAT, 128), 1) < DR
    low_r = iota((DR, 128), 1) < DR

    def stationary(i, lat_i, rp):
        rr = rp + pltpu.roll(rp, DR, 1)
        cos = jnp.concatenate([cs[i, 0]] * 8, axis=0)
        sin = jnp.concatenate([cs[i, 1]] * 8, axis=0)
        rr = rr * cos + pltpu.roll(rr, DR // 2, 1) * sin
        lat_t = jnp.transpose(jnp.concatenate([lat_i, lat_i], axis=0))
        rr_t = jnp.transpose(jnp.concatenate([rr, rr], axis=0))[:DR]
        left = jnp.where(low_q, lat_t, 0.0).astype(BF16)
        right = jnp.where(low_q, 0.0, lat_t).astype(BF16)
        rleft = jnp.where(low_r, rr_t, 0.0).astype(BF16)
        rright = jnp.where(low_r, 0.0, rr_t).astype(BF16)
        wqt[i, 0:512, 0:128] = left
        wqt[i, 512:1024, 0:128] = right
        wqt[i, 1024:1536, 128:256] = left
        wqt[i, 1536:2048, 128:256] = right
        wqt[i, 2048:2112, 0:128] = rleft
        wqt[i, 2112:2176, 0:128] = rright
        wqt[i, 2176:2240, 128:256] = rleft
        wqt[i, 2240:2304, 128:256] = rright

    def queries(n):
        q_wait(n).wait_recv()
        dst = qparts[n][1]
        got = jnp.dot(perm, dst[...].reshape(GROUP * 16, dst.shape[2]), preferred_element_type=F32)

        def build(i):
            m = i - 2 * n
            if m < 2:
                left = got[64 * m : 64 * m + 64, :256]
                right = got[128 + 64 * m : 192 + 64 * m, :256]
                stationary(i, jnp.concatenate([left, right], axis=1), got[64 * m : 64 * m + 64, 256:384])
            else:
                lat_i = jnp.concatenate([got[64 * j : 64 * j + 64, 384:512] for j in range(4)], axis=1)
                stationary(i, lat_i, got[128:192, 256:384])

        return build

    build = queries(0)
    build(0)
    v_wait_all(0)
    v_start(1)
    pool_copy.wait()

    def page(i, c, k, g):
        return bt[i, c * 16 + k * 4 + g]

    def keys(i, c, k):
        return jnp.concatenate([pool[page(i, c, k, g)] for g in range(4)], axis=0)

    def scores(i, buf, slot, chunks):
        size = 256 * len(chunks)
        low = iota((64, 128), 1) < DR

        def latents(k):
            return jnp.concatenate([pool[page(i, c, k, g)] for c in chunks for g in range(4)], axis=0)

        def rotary(e):
            return jnp.concatenate(
                [
                    jnp.where(low, zpool[page(i, c, 2 * e, g)], zpool[page(i, c, 2 * e + 1, g)])
                    for c in chunks
                    for g in range(4)
                ],
                axis=0,
            )

        lhs = jnp.concatenate([latents(k) for k in range(4)] + [rotary(0), rotary(1)], axis=1)
        s = jnp.dot(lhs, wqt[i], preferred_element_type=F32)
        token = iota((256, 256), 0) + (iota((256, 256), 1) // 64) * 256
        m = m_sc[slot]
        for n, c in enumerate(chunks):
            part = jnp.where(token < ln[i] - c * 1024, s[256 * n : 256 * n + 256], NEG)
            buf[256 * c : 256 * c + 256, :] = part
            m = jnp.maximum(m, jnp.max(part.reshape(32, 8, 256), axis=0))
        m_sc[slot] = m

    def fresh(i, buf, slot):
        new = jnp.concatenate([nef[i], jnp.zeros((8, 640), F32)], axis=0).astype(BF16)
        s = jnp.dot(new[:, :LAT], wqt[i, 0:512], preferred_element_type=F32)
        s = s + jnp.dot(new[:, LAT:], wqt[i, 2048:2176], preferred_element_type=F32)
        u = iota((16, 256), 0)
        lane = iota((16, 256), 1)
        s = jnp.where((lane < 64) & (u <= lax.rem(lane, STEPS)), s, NEG)
        buf[1024:1040, :] = s
        m_sc[slot] = jnp.maximum(s[0:8], s[8:16])

    def top(slot):
        m = jnp.max(m_sc[slot], axis=0, keepdims=True)
        m = jnp.broadcast_to(m, (8, 256))
        m = jnp.maximum(m, pltpu.roll(m, 128, 1))
        m = jnp.maximum(m, pltpu.roll(m, 64, 1))
        return m

    def weigh(i, buf, slot):
        def chunk(c):
            s = buf[256 * c : 256 * c + 256, :]
            p = jnp.exp2((s - m_sc[slot][0:1]) * SCALE)
            l_sc[...] = l_sc[...] + jnp.sum(p.reshape(32, 8, 256), axis=0)
            pt = jnp.transpose(p).astype(BF16)
            t = acc[...]
            for k in range(4):
                t = t + jnp.dot(pt[64 * k : 64 * k + 64], keys(i, c, k), preferred_element_type=F32)
            acc[...] = t

        return chunk

    def weigh_fresh(i, buf, slot):
        s = buf[1024:1040, :]
        p = jnp.exp2((s - m_sc[slot][0:1]) * SCALE)
        l_sc[...] = p[0:8] + p[8:16]
        pt = jnp.transpose(jnp.concatenate([p[:, 0:128], jnp.zeros((112, 128), F32)], axis=0)).astype(BF16)
        new = jnp.concatenate([nef[i, :, :LAT], jnp.zeros((120, LAT), F32)], axis=0).astype(BF16)
        acc[...] = jnp.dot(pt[:64], new, preferred_element_type=F32)

    def finish(i):
        total = jnp.sum(l_sc[...], axis=0, keepdims=True)
        total = jnp.broadcast_to(total, (8, 256))
        total = total + pltpu.roll(total, 128, 1)
        total = total + pltpu.roll(total, 64, 1)
        col = jnp.transpose(jnp.broadcast_to(1.0 / total[0:1, :128], (128, 128)))[:64, 0:1]
        att[i] = acc[...] * col

    def forward():
        v_wait_all(1)
        pltpu.make_async_remote_copy(
            src_ref=vfull.at[:, :, core], dst_ref=vfull.at[:, :, core], send_sem=vc_sem.at[0], recv_sem=vc_sem.at[1],
            device_id={"rep": other}, device_id_type=MESH,
        ).start()

    bufs = (s_a, s_b)
    for i in range(REQ + 1):
        if i == 2:
            build = queries(1)
        if 0 < i < REQ:
            build(i)
        if i < REQ:
            fresh(i, bufs[i % 2], i % 2)
        if i > 0:
            m_sc[(i - 1) % 2] = top((i - 1) % 2)
            weigh_fresh(i - 1, bufs[(i - 1) % 2], (i - 1) % 2)

        for c in range(0, 4, GATHER):
            if i < REQ:
                scores(i, bufs[i % 2], i % 2, list(range(c, c + GATHER)))
            if i > 0:
                for d in range(c, c + GATHER):
                    weigh(i - 1, bufs[(i - 1) % 2], (i - 1) % 2)(d)
        if i > 0:
            finish(i - 1)
        if i == 3:
            forward()

    q_wait(0).wait_send()
    q_wait(1).wait_send()
    for hop in range(2):
        for side in range(2):
            for k in range(1, 4):
                v_copy(hop, side, k).wait_send()

    pltpu.make_async_remote_copy(
        src_ref=vfull.at[:, :, 1 - core], dst_ref=vfull.at[:, :, 1 - core], send_sem=vc_sem.at[0], recv_sem=vc_sem.at[1],
        device_id={"rep": other}, device_id_type=MESH,
    ).wait_recv()
    for p in range(HEADS // 2):
        rows = att[:, 8 * p : 8 * p + 8, :].reshape(REQ * 8, LAT).astype(BF16)
        v = vfull[:, :, :, :, 256 * p : 256 * p + 256].reshape(LAT, 256)
        o = jnp.dot(rows, v, preferred_element_type=F32).reshape(REQ, 8, 256)
        for i in range(REQ):
            out_ref[i, :, 256 * p : 256 * p + 128] = o[i, 0:4, 0:128].astype(BF16)
            out_ref[i, :, 256 * p + 128 : 256 * p + 256] = o[i, 4:8, 128:256].astype(BF16)

    pltpu.make_async_remote_copy(
        src_ref=vfull.at[:, :, core], dst_ref=vfull.at[:, :, core], send_sem=vc_sem.at[0], recv_sem=vc_sem.at[1],
        device_id={"rep": other}, device_id_type=MESH,
    ).wait_send()


def on_device(query_latent, new_entry, cache_latent, cache_rope, block_table, context_len, owner_rows, query_up, key_up, value_up):
    half = DR // 2
    freq = np.float32(10000.0) ** (-np.arange(half, dtype=np.float32) / np.float32(half))
    freq = jnp.asarray(np.tile(freq, 4).reshape(1, 128).astype(np.float32))
    vmem = pl.BlockSpec(memory_space=pltpu.VMEM)
    smem = pl.BlockSpec(memory_space=pltpu.SMEM)
    hbm = pl.BlockSpec(memory_space=pl.ANY)
    dma = pltpu.SemaphoreType.DMA
    out = pl.pallas_call(
        kernel,
        out_shape=jax.ShapeDtypeStruct((REQ, STEPS, HEADS * DN), BF16),
        in_specs=[vmem, vmem, hbm, hbm, smem, smem, smem, hbm, hbm, hbm, vmem],
        out_specs=vmem,
        scratch_shapes=[
            pltpu.VMEM((POOL, 64, LAT), BF16),
            pltpu.VMEM((POOL, 64, 128), BF16),
            pltpu.VMEM((POOL, 4096), BF16),
            pltpu.VMEM((XN, 12, 3072), BF16),
            pltpu.VMEM((XN, 4, 2048), BF16),
            pltpu.VMEM((XN, 4, 2048), BF16),
            pltpu.VMEM((48, 3072), F32),
            pltpu.VMEM((16, 2048), F32),
            pltpu.VMEM((HEADS, MSG, 128), BF16),
            pltpu.VMEM((REP, MSG, 128), BF16),
            pltpu.VMEM((4, 4, 2, 16, 2048), BF16),
            pltpu.VMEM((16, XW), F32),
            pltpu.VMEM((2, 4, 2, 16, XW), BF16),
            pltpu.VMEM((GROUP, 32, QR), BF16),
            pltpu.VMEM((QR, 256), BF16),
            pltpu.VMEM((GROUP, 16, 384), BF16),
            pltpu.VMEM((GROUP, 16, 384), BF16),
            pltpu.VMEM((GROUP, 16, 512), BF16),
            pltpu.VMEM((GROUP, 16, 512), BF16),
            pltpu.VMEM((REQ, 2304, 256), BF16),
            pltpu.VMEM((1040, 256), F32),
            pltpu.VMEM((1040, 256), F32),
            pltpu.VMEM((2, 8, 256), F32),
            pltpu.VMEM((8, 256), F32),
            pltpu.VMEM((64, LAT), F32),
            pltpu.VMEM((REQ, 64, LAT), F32),
            pltpu.VMEM((REQ, 8, 640), F32),
            pltpu.VMEM((REQ, 2, 8, 128), F32),
            pltpu.VMEM((512, 256), BF16),
            pltpu.SMEM((REP,), jnp.int32),
            dma((2,)), dma((4,)), dma((4, XN)), dma((4, XN)),
            dma((2, 2, 4)), dma((2, 2, 4)), dma((2,)), dma((1,)), dma((1,)),
            dma((2, 2, 4)), dma((2, 2, 4)), dma((2,)), dma((2,)), dma((2,)),
            pltpu.SemaphoreType.REGULAR, pltpu.SemaphoreType.REGULAR,
        ],
        compiler_params=pltpu.CompilerParams(
            collective_id=0, has_side_effects=True, vmem_limit_bytes=60 * 2**20
        ),
        name="latent_attention",
    )(jnp.swapaxes(query_latent, 0, 1), jnp.swapaxes(new_entry, 0, 1), cache_latent, cache_rope, block_table, context_len, owner_rows, query_up, key_up, value_up, freq)
    return jnp.swapaxes(out, 0, 1)


def solution(mesh):
    return jax.shard_map(
        on_device,
        mesh=mesh,
        in_specs=(
            P(None, "rep", None),
            P(None, "rep", None),
            P("rep", None, None),
            P("rep", None),
            P("rep", None),
            P("rep"),
            P(),
            P(("rep", "head"), None),
            P(("rep", "head"), None),
            P(("rep", "head"), None),
        ),
        out_specs=P(None, "rep", "head"),
        check_vma=False,
    )
```
